32 devices in a mesh: dp: 4 (over y, x), shard: 8 (over z, core).
Axes of the slice: x: 2, y: 2, z: 4, core: 2. Of those that a mesh axis runs over, the one named last changes fastest.
Arguments:
- tokens: bfloat16 [8192, 1600], P(('dp', 'shard')), may hold values from -6 to 6
- cotangent: bfloat16 [8192, 1600], P(('dp', 'shard')), may hold values from -6 to 6
- lengths: int32 [32, 2], P(('dp', 'shard')), may hold values from 0 to 256, as said below
- step_count: int32 [1], replicated, may hold values from 1 to 20
- norm_gains: bfloat16 [1600, 4], P('shard'), may hold values from 0.5 to 1.5
- qkv_weight: bfloat16 [1600, 2240], P('shard', 'dp'), may hold values from -0.15625 to 0.15625
- attn_weight: bfloat16 [1600, 1600], P('shard', 'dp'), may hold values from -0.15625 to 0.15625
- mixer_in: bfloat16 [1600, 6400], P('shard', 'dp'), may hold values from -0.15625 to 0.15625
- mixer_table: bfloat16 [3200, 255], P('shard'), may hold values from -7 to 3
- mixer_out: bfloat16 [3200, 1600], P('shard', 'dp'), may hold values from -0.109375 to 0.109375
- ffn_in: bfloat16 [1600, 11008], P('shard', 'dp'), may hold values from -0.15625 to 0.15625
- ffn_out: bfloat16 [5504, 1600], P('shard', 'dp'), may hold values from -0.078125 to 0.078125
- first_gains: float32 [1600, 4], P('shard'), may hold values from -16 to 16
- first_qkv: float32 [1600, 2240], P('shard', 'dp'), may hold values from -16 to 16
- first_attn: float32 [1600, 1600], P('shard', 'dp'), may hold values from -16 to 16
- first_mixin: float32 [1600, 6400], P('shard', 'dp'), may hold values from -16 to 16
- first_table: float32 [3200, 255], P('shard'), may hold values from -16 to 16
- first_mixout: float32 [3200, 1600], P('shard', 'dp'), may hold values from -16 to 16
- first_ffnin: float32 [1600, 11008], P('shard', 'dp'), may hold values from -16 to 16
- first_ffnout: float32 [5504, 1600], P('shard', 'dp'), may hold values from -16 to 16
- second_gains: float32 [1600, 4], P('shard'), may hold values from 20 to 500
- second_qkv: float32 [1600, 2240], P('shard', 'dp'), may hold values from 20 to 500
- second_attn: float32 [1600, 1600], P('shard', 'dp'), may hold values from 20 to 500
- second_mixin: float32 [1600, 6400], P('shard', 'dp'), may hold values from 20 to 500
- second_table: float32 [3200, 255], P('shard'), may hold values from 20 to 500
- second_mixout: float32 [3200, 1600], P('shard', 'dp'), may hold values from 20 to 500
- second_ffnin: float32 [1600, 11008], P('shard', 'dp'), may hold values from 20 to 500
- second_ffnout: float32 [5504, 1600], P('shard', 'dp'), may hold values from 20 to 500
Outputs:
- output: bfloat16 [8192, 1600], P(('dp', 'shard'))
- grad_tokens: float32 [8192, 1600], P(('dp', 'shard'))
- grad_gains: float32 [1600, 4], P('shard')
- grad_qkv: float32 [1600, 2240], P('shard', 'dp')
- grad_attn: float32 [1600, 1600], P('shard', 'dp')
- grad_mixin: float32 [1600, 6400], P('shard', 'dp')
- grad_table: float32 [3200, 255], P('shard')
- grad_mixout: float32 [3200, 1600], P('shard', 'dp')
- grad_ffnin: float32 [1600, 11008], P('shard', 'dp')
- grad_ffnout: float32 [5504, 1600], P('shard', 'dp')
- mean_gains: float32 [1600, 4], P('shard')
- mean_qkv: float32 [1600, 2240], P('shard', 'dp')
- mean_attn: float32 [1600, 1600], P('shard', 'dp')
- mean_mixin: float32 [1600, 6400], P('shard', 'dp')
- mean_table: float32 [3200, 255], P('shard')
- mean_mixout: float32 [3200, 1600], P('shard', 'dp')
- mean_ffnin: float32 [1600, 11008], P('shard', 'dp')
- mean_ffnout: float32 [5504, 1600], P('shard', 'dp')
- square_gains: float32 [1600, 4], P('shard')
- square_qkv: float32 [1600, 2240], P('shard', 'dp')
- square_attn: float32 [1600, 1600], P('shard', 'dp')
- square_mixin: float32 [1600, 6400], P('shard', 'dp')
- square_table: float32 [3200, 255], P('shard')
- square_mixout: float32 [3200, 1600], P('shard', 'dp')
- square_ffnin: float32 [1600, 11008], P('shard', 'dp')
- square_ffnout: float32 [5504, 1600], P('shard', 'dp')
- delta_gains: float32 [1600, 4], P('shard')
- delta_qkv: float32 [1600, 2240], P('shard', 'dp')
- delta_attn: float32 [1600, 1600], P('shard', 'dp')
- delta_mixin: float32 [1600, 6400], P('shard', 'dp')
- delta_table: float32 [3200, 255], P('shard')
- delta_mixout: float32 [3200, 1600], P('shard', 'dp')
- delta_ffnin: float32 [1600, 11008], P('shard', 'dp')
- delta_ffnout: float32 [5504, 1600], P('shard', 'dp')
The draws below stay inside these ranges and needn't reach their ends.
Inputs may be any that keep to these rules, and one draw needn't show every extreme that they name: Row i lists the lengths of buffer i's sequences in order, zeros after the last; each sequence is padded to whole blocks of 128 rows and a row's blocks add up to at most 2. In every draw some row holds one sequence of 256 rows.
All inputs are finite; a program needn't handle non-finite values.
Results may differ from the reference program's by a relative error of at most 0.014.
Values may be sent and summed in bfloat16 or wider, within the bound.
A program may use at most 512 MiB of HBM per device.

```python
import math
import jax
import jax.numpy as jnp
from jax import lax

D = 1600
KV = 5
HEAD = 64
GROUP = 5
INNER = 3200
STATE = 16
CONV = 4
RANK = 100
FF = 5504
BLOCK = 128
BLOCKS = 2
CAP = 256
TOKENS = 8192
TABLE = 255
QKVW = 2240
N_DP = 4
N_SHARD = 8


def draw_step_count(key, part):
    return jax.random.randint(jax.random.fold_in(key, 37), (1,), 1, 21).astype(jnp.int32)


def draw_lengths(key, part):
    device_count = TOKENS // CAP
    keys = jax.random.split(jax.random.fold_in(key, 11), 4)
    lowest = max(1, (BLOCKS + 1) // 2)
    used = jax.random.randint(keys[0], (device_count,), lowest, BLOCKS + 1)
    fresh = jax.random.randint(keys[1], (device_count, BLOCKS), 0, 2)
    index = jnp.arange(BLOCKS, dtype=jnp.int32)
    leading = (index[None, :] == 0).astype(jnp.int32)
    fresh = jnp.where(index[None, :] == 0, 1, fresh)
    chosen = jax.random.randint(keys[3], (), 0, device_count)
    device = jnp.arange(device_count, dtype=jnp.int32)
    full_row = device == chosen
    used = jnp.where(full_row, BLOCKS, used)
    fresh = jnp.where(full_row[:, None], leading, fresh)
    live_block = index[None, :] < used[:, None]
    owner = jnp.cumsum(fresh * live_block.astype(jnp.int32), axis=1) - 1
    blocks_per = jnp.sum(((owner[:, :, None] == index[None, None, :]) & live_block[:, :, None]).astype(jnp.int32), axis=1)
    tail = jax.random.randint(keys[2], (device_count, BLOCKS), 1, BLOCK + 1)
    tail = jnp.where(full_row[:, None], BLOCK, tail)
    return jnp.where(blocks_per > 0, (blocks_per - 1) * BLOCK + tail, 0).astype(jnp.int32)


def draw_mixer_table(key, part):
    keys = jax.random.split(jax.random.fold_in(key, 23), 7)
    taps = jax.random.truncated_normal(keys[0], -3.0, 3.0, (INNER, CONV), jnp.float32) * 0.5
    conv_bias = jax.random.uniform(keys[1], (INNER, 1), jnp.float32, -0.5, 0.5)
    step_rate = jnp.exp(jax.random.uniform(keys[2], (INNER, 1), jnp.float32, math.log(0.001), math.log(0.1)))
    step_bias = step_rate + jnp.log(-jnp.expm1(-step_rate))
    skip_weight = jax.random.uniform(keys[3], (INNER, 1), jnp.float32, 0.5, 1.5)
    log_rates = jax.random.uniform(keys[4], (INNER, STATE), jnp.float32, 0.0, math.log(16.0))
    input_proj = jax.random.truncated_normal(keys[5], -3.0, 3.0, (INNER, RANK + 2 * STATE), jnp.float32) * INNER ** (-0.5)
    step_proj = jax.random.truncated_normal(keys[6], -3.0, 3.0, (INNER, RANK), jnp.float32) * RANK ** (-0.5)
    table = jnp.concatenate([taps, conv_bias, step_bias, skip_weight, log_rates, input_proj, step_proj], axis=1)
    return table.astype(jnp.bfloat16)


def block_scale(rng, dims, cuts, smallest, top_value):
    level, own = 1.0, jax.random.fold_in(rng, 6)
    for dim, shards_of in cuts:
        steps = jnp.exp(jax.random.uniform(jax.random.fold_in(own, dim), (shards_of,), jnp.float32, smallest / len(cuts), top_value / len(cuts)))
        level = level * jnp.repeat(steps, dims[dim] // shards_of).reshape([-1 if axis == dim else 1 for axis in range(len(dims))])
    return level


def gaussian(key, dims, width, most, cuts=(), kind=jnp.bfloat16):
    loudness = block_scale(key, dims, cuts, -0.22, 0.18) if cuts else 1.0
    array = jax.random.normal(key, dims, jnp.float32) * width * loudness
    return jnp.minimum(jnp.maximum(array, -most), most).astype(kind)


def setup_inputs(seed: int = 0) -> dict:
    key_of = jax.random.split(jax.random.key(seed), 29)
    return {
        "tokens": gaussian(key_of[0], (TOKENS, D), 1.0, 6.0, ((0, 32),)),
        "cotangent": gaussian(key_of[1], (TOKENS, D), 1.0, 6.0, ((0, 32),)),
        "lengths": draw_lengths(jax.random.fold_in(key_of[28], 71), 0),
        "step_count": draw_step_count(jax.random.fold_in(key_of[28], 71), 0),
        "norm_gains": jnp.clip(1.0 + 0.1 * jax.random.normal(key_of[4], (D, 4), jnp.float32), 0.5, 1.5).astype(jnp.bfloat16),
        "qkv_weight": gaussian(key_of[5], (D, QKVW), D ** -0.5, 0.15625, ((0, 8), (1, 4))),
        "attn_weight": gaussian(key_of[6], (D, D), D ** -0.5, 0.15625, ((0, 8), (1, 4))),
        "mixer_in": gaussian(key_of[7], (D, 2 * INNER), D ** -0.5, 0.15625, ((0, 8), (1, 4))),
        "mixer_table": draw_mixer_table(jax.random.fold_in(key_of[28], 71), 0),
        "mixer_out": gaussian(key_of[9], (INNER, D), INNER ** -0.5, 0.109375, ((0, 8), (1, 4))),
        "ffn_in": gaussian(key_of[10], (D, 2 * FF), D ** -0.5, 0.15625, ((0, 8), (1, 4))),
        "ffn_out": gaussian(key_of[11], (FF, D), FF ** -0.5, 0.078125, ((0, 8), (1, 4))),
        "first_gains": gaussian(key_of[12], (D, 4), 4.0, 16.0, ((0, 8),), jnp.float32),
        "first_qkv": gaussian(key_of[13], (D, QKVW), 4.0, 16.0, ((0, 8), (1, 4)), jnp.float32),
        "first_attn": gaussian(key_of[14], (D, D), 4.0, 16.0, ((0, 8), (1, 4)), jnp.float32),
        "first_mixin": gaussian(key_of[15], (D, 2 * INNER), 4.0, 16.0, ((0, 8), (1, 4)), jnp.float32),
        "first_table": gaussian(key_of[16], (INNER, TABLE), 4.0, 16.0, ((0, 8),), jnp.float32),
        "first_mixout": gaussian(key_of[17], (INNER, D), 4.0, 16.0, ((0, 8), (1, 4)), jnp.float32),
        "first_ffnin": gaussian(key_of[18], (D, 2 * FF), 4.0, 16.0, ((0, 8), (1, 4)), jnp.float32),
        "first_ffnout": gaussian(key_of[19], (FF, D), 4.0, 16.0, ((0, 8), (1, 4)), jnp.float32),
        "second_gains": jnp.clip(jnp.exp(math.log(500.0) - 3.218876 * jax.random.uniform(key_of[20], (D, 4), jnp.float32) ** block_scale(key_of[20], (D, 4), ((0, 8),), -0.2, 0.2)), 20.0, 500.0),
        "second_qkv": jnp.clip(jnp.exp(math.log(500.0) - 3.218876 * jax.random.uniform(key_of[21], (D, QKVW), jnp.float32) ** block_scale(key_of[21], (D, QKVW), ((0, 8), (1, 4)), -0.2, 0.2)), 20.0, 500.0),
        "second_attn": jnp.clip(jnp.exp(math.log(500.0) - 3.218876 * jax.random.uniform(key_of[22], (D, D), jnp.float32) ** block_scale(key_of[22], (D, D), ((0, 8), (1, 4)), -0.2, 0.2)), 20.0, 500.0),
        "second_mixin": jnp.clip(jnp.exp(math.log(500.0) - 3.218876 * jax.random.uniform(key_of[23], (D, 2 * INNER), jnp.float32) ** block_scale(key_of[23], (D, 2 * INNER), ((0, 8), (1, 4)), -0.2, 0.2)), 20.0, 500.0),
        "second_table": jnp.clip(jnp.exp(math.log(500.0) - 3.218876 * jax.random.uniform(key_of[24], (INNER, TABLE), jnp.float32) ** block_scale(key_of[24], (INNER, TABLE), ((0, 8),), -0.2, 0.2)), 20.0, 500.0),
        "second_mixout": jnp.clip(jnp.exp(math.log(500.0) - 3.218876 * jax.random.uniform(key_of[25], (INNER, D), jnp.float32) ** block_scale(key_of[25], (INNER, D), ((0, 8), (1, 4)), -0.2, 0.2)), 20.0, 500.0),
        "second_ffnin": jnp.clip(jnp.exp(math.log(500.0) - 3.218876 * jax.random.uniform(key_of[26], (D, 2 * FF), jnp.float32) ** block_scale(key_of[26], (D, 2 * FF), ((0, 8), (1, 4)), -0.2, 0.2)), 20.0, 500.0),
        "second_ffnout": jnp.clip(jnp.exp(math.log(500.0) - 3.218876 * jax.random.uniform(key_of[27], (FF, D), jnp.float32) ** block_scale(key_of[27], (FF, D), ((0, 8), (1, 4)), -0.2, 0.2)), 20.0, 500.0),
    }


epsilon = 1e-06
highest = lax.Precision.HIGHEST
beta_first = 0.9
beta_second = 0.95
adam_floor = 1e-08
learn_rate = 0.01
weight_decay = 0.1
masked_score = -1e+30

@jax.custom_vjp
def low(v):
    return lax.optimization_barrier(v.astype(jnp.bfloat16)).astype(jnp.float32)

@jax.custom_vjp
def low_back(v):
    return v

def low_keep(v):
    return (low(v), None)

def low_pass(kept, grad):
    return (grad,)

def back_keep(v):
    return (v, None)

def back_low(kept, grad):
    return (low(grad),)
low.defvjp(low_keep, low_pass)
low_back.defvjp(back_keep, back_low)

def matmul(left, right):
    return jnp.dot(left, right, precision=highest, preferred_element_type=jnp.float32)

def silu_act(values):
    return values / (1.0 + jnp.exp(-values))

def rms_norm(values, gain):
    return values * lax.rsqrt(lax.optimization_barrier(jnp.mean(values * values, axis=-1, keepdims=True)) + epsilon) * gain

def shift_rows(values, lag):
    if lag == 0:
        return values
    return jnp.concatenate([jnp.zeros((lag, values.shape[1]), values.dtype), values[:values.shape[0] - lag]], axis=0)

def layout(row):
    index = jnp.arange(BLOCKS, dtype=jnp.int32)
    count_blocks = ((row + (BLOCK - 1)) // BLOCK).astype(jnp.int32)
    first_block = (jnp.cumsum(count_blocks) - count_blocks).astype(jnp.int32)
    places = jnp.arange(CAP, dtype=jnp.int32)
    owner = lax.optimization_barrier(jnp.sum((first_block[None, :] <= (places // BLOCK)[:, None]).astype(jnp.int32), axis=1)).astype(jnp.int32) - 1
    pick = (owner[:, None] == index[None, :]).astype(jnp.int32)
    seq_length = lax.optimization_barrier(jnp.sum(pick * row[None, :], axis=1)).astype(jnp.int32)
    offset = (places - BLOCK * lax.optimization_barrier(jnp.sum(pick * first_block[None, :], axis=1))).astype(jnp.int32)
    live = offset < seq_length
    begins = live & (offset == 0)
    allowed = (owner[:, None] == owner[None, :]) & (places[None, :] <= places[:, None]) & live[None, :] | (places[:, None] == places[None, :])
    return (offset, live.astype(jnp.float32), 1.0 - begins.astype(jnp.float32), allowed)

def attention(heads, allowed):
    query = heads[:, :D].reshape(CAP, KV, GROUP, HEAD)
    key_rows = heads[:, D:D + KV * HEAD].reshape(CAP, KV, HEAD)
    value_rows = heads[:, D + KV * HEAD:].reshape(CAP, KV, HEAD)
    scores = jnp.einsum('qkgd,skd->kgqs', query, key_rows, precision=highest) * HEAD ** (-0.5)
    scores = low_back(scores)
    scores = jnp.where(allowed, scores, masked_score)
    top_score = lax.optimization_barrier(jnp.max(scores, axis=-1, keepdims=True))
    log_total = top_score + jnp.log(lax.optimization_barrier(jnp.sum(jnp.exp(scores - top_score), axis=-1, keepdims=True)))
    probs = low(jnp.exp(scores - log_total))
    context = jnp.einsum('kgqs,skd->qkgd', probs, value_rows, precision=highest).reshape(CAP, D)
    return low(low_back(context))

def mamba(normed, weight_in, table, weight_mix, offset, keep_rows):
    mixed = low_back(matmul(normed, weight_in))
    xin = mixed[:, :INNER]
    gate_z = mixed[:, INNER:]
    conv_pre = table[:, CONV]
    for lag in range(CONV):
        conv_pre = conv_pre + table[:, lag] * (shift_rows(xin, lag) * (offset >= lag).astype(jnp.float32)[:, None])
    conv_out = low(silu_act(conv_pre))
    proj_start = CONV + 3 + STATE
    double = low_back(matmul(conv_out, table[:, proj_start:proj_start + RANK + 2 * STATE]))
    rank_part = low(double[:, :RANK])
    inject = double[:, RANK:RANK + STATE]
    readout = double[:, RANK + STATE:]
    dt_pre = low_back(matmul(rank_part, table[:, proj_start + RANK + 2 * STATE:].T)) + table[:, CONV + 1]
    step_size = jnp.log1p(jnp.exp(dt_pre))
    rates = -jnp.exp(table[:, CONV + 3:CONV + 3 + STATE]).T
    decay = jnp.exp(step_size[:, None, :] * rates[None]) * keep_rows[:, None, None]
    drive = (step_size * conv_out)[:, None, :] * inject[:, :, None]

    def advance(state, item):
        fade, push, read = item
        state = fade * state + push
        return (state, lax.optimization_barrier(jnp.sum(state * read[:, None], axis=0)))
    final_state, scanned = lax.scan(jax.checkpoint(advance), jnp.zeros((STATE, INNER), jnp.float32), (decay, drive, readout))
    scanned = scanned + table[:, CONV + 2] * conv_out
    gated = low(scanned * silu_act(gate_z))
    return low_back(matmul(gated, weight_mix))

def forward(inputs, weights, info):
    gain_cols, weight_qkv, weight_attn, weight_in, table, weight_mix, weight_up, weight_down = weights
    offset, live_rows, keep_rows, allowed = info
    normed = low(rms_norm(inputs, gain_cols[:, 0]))
    heads = low(low_back(matmul(normed, weight_qkv)))
    attn_raw = low_back(matmul(attention(heads, allowed), weight_attn))
    mamba_raw = mamba(normed, weight_in, table, weight_mix, offset, keep_rows)
    hidden = inputs + 0.5 * (rms_norm(attn_raw, gain_cols[:, 1]) + rms_norm(mamba_raw, gain_cols[:, 2]))
    normed_two = low(rms_norm(hidden, gain_cols[:, 3]))
    both = low_back(matmul(normed_two, weight_up))
    act = low(silu_act(both[:, :FF]) * both[:, FF:])
    ffn_raw = low_back(matmul(act, weight_down))
    return live_rows[:, None] * (hidden + ffn_raw)

def adam_update(weight, gradient, first_old, second_old, step_float):
    mean_new = beta_first * first_old + (1.0 - beta_first) * gradient
    square_new = beta_second * second_old + (1.0 - beta_second) * gradient * gradient
    fix_first = 1.0 - jnp.power(beta_first, step_float)
    fix_second = 1.0 - jnp.power(beta_second, step_float)
    delta_new = -learn_rate * (mean_new / fix_first / (jnp.sqrt(square_new / fix_second) + adam_floor) + weight_decay * weight)
    return (mean_new, square_new, delta_new)

def reference(tokens, cotangent, lengths, step_count, norm_gains, qkv_weight, attn_weight, mixer_in, mixer_table, mixer_out, ffn_in, ffn_out, first_gains, first_qkv, first_attn, first_mixin, first_table, first_mixout, first_ffnin, first_ffnout, second_gains, second_qkv, second_attn, second_mixin, second_table, second_mixout, second_ffnin, second_ffnout):
    weights = tuple((item.astype(jnp.float32) for item in (norm_gains, qkv_weight, attn_weight, mixer_in, mixer_table, mixer_out, ffn_in, ffn_out)))
    firsts = (first_gains, first_qkv, first_attn, first_mixin, first_table, first_mixout, first_ffnin, first_ffnout)
    seconds = (second_gains, second_qkv, second_attn, second_mixin, second_table, second_mixout, second_ffnin, second_ffnout)
    device_count = N_DP * N_SHARD
    row_blocks = tokens.astype(jnp.float32).reshape(device_count, CAP, D)
    cot_blocks = cotangent.astype(jnp.float32).reshape(device_count, CAP, D)

    def visit(totals, item):
        inputs, cot_rows, row = item
        info = layout(row)

        def run(inputs, *params):
            return forward(inputs, params, info)
        result, pull = jax.vjp(run, inputs, *weights)
        grads = pull(cot_rows)
        return (tuple((acc + part for acc, part in zip(totals, grads[1:]))), (result, grads[0]))
    totals, (results, grad_rows) = lax.scan(visit, tuple((jnp.zeros_like(item) for item in weights)), (row_blocks, cot_blocks, lengths))
    step_float = step_count[0].astype(jnp.float32)
    updates = [adam_update(weights[slot], totals[slot], firsts[slot], seconds[slot], step_float) for slot in range(8)]
    output = results.reshape(TOKENS, D).astype(jnp.bfloat16)
    grad_tokens = grad_rows.reshape(TOKENS, D)
    return (output, grad_tokens, totals[0], totals[1], totals[2], totals[3], totals[4], totals[5], totals[6], totals[7], updates[0][0], updates[1][0], updates[2][0], updates[3][0], updates[4][0], updates[5][0], updates[6][0], updates[7][0], updates[0][1], updates[1][1], updates[2][1], updates[3][1], updates[4][1], updates[5][1], updates[6][1], updates[7][1], updates[0][2], updates[1][2], updates[2][2], updates[3][2], updates[4][2], updates[5][2], updates[6][2], updates[7][2])
```

```python
import functools

import jax
import jax.numpy as jnp
from jax import lax
from jax.experimental import pallas as pl
from jax.experimental.pallas import tpu as pltpu
from jax.sharding import PartitionSpec as P

KV = 5
HEAD = 64
GROUP = 5
INNER = 3200
STATE = 16
CONV = 4
RANK = 100
FF = 5504
BLOCK = 128
CHUNK = 32


epsilon = 1e-06
beta_first = 0.9
beta_second = 0.95
adam_floor = 1e-08
learn_rate = 0.01
weight_decay = 0.1
masked_score = -1e30


def product(left, right):
    return jnp.dot(left, right, preferred_element_type=jnp.float32)


def product_tn(left, right):
    return lax.dot_general(
        left, right, (((0,), (0,)), ((), ())), preferred_element_type=jnp.float32
    )


def product_nt(left, right):
    return lax.dot_general(
        left, right, (((1,), (1,)), ((), ())), preferred_element_type=jnp.float32
    )


def sigmoid(values):
    return 1.0 / (1.0 + jnp.exp(-values))


def silu_act(values):
    return values / (1.0 + jnp.exp(-values))


def silu_slope(values):
    gate_sig = sigmoid(values)
    return gate_sig * (1.0 + values * (1.0 - gate_sig))


def rms_scale(values):
    return lax.rsqrt(jnp.mean(values * values, axis=-1, keepdims=True) + epsilon)


def rms_back(values, scale, gain, incoming):
    weighted = incoming * gain
    inner_mean = jnp.mean(weighted * values, axis=-1, keepdims=True)
    return (
        scale * weighted - values * (scale * scale * scale) * inner_mean,
        jnp.sum(incoming * values * scale, axis=0),
    )


def shift_rows(values, lag):
    if lag == 0:
        return values
    return jnp.concatenate(
        [jnp.zeros((lag, values.shape[1]), values.dtype), values[: values.shape[0] - lag]], axis=0
    )


def unshift_rows(values, lag):
    if lag == 0:
        return values
    return jnp.concatenate([values[lag:], jnp.zeros((lag, values.shape[1]), values.dtype)], axis=0)


LANES=128

def row_sums(parts):
    rows = lax.broadcasted_iota(jnp.int32, (8, LANES), 0)
    quads = []
    low = rows < 4
    for i in range(4):
        a, b = parts[i], parts[i + 4]
        quads.append(jnp.where(low, a, b) + pltpu.roll(jnp.where(low, b, a), 4, 0))
    pairs = []
    low = (rows & 3) < 2
    for i in range(2):
        a, b = quads[i], quads[i + 2]
        pairs.append(jnp.where(low, a + pltpu.roll(a, 6, 0), b + pltpu.roll(b, 2, 0)))
    a, b = pairs
    return jnp.where((rows & 1) < 1, a + pltpu.roll(a, 7, 0), b + pltpu.roll(b, 1, 0))

def fold(values):
    return values[:8] + values[8:]

def scan_kernel(per_block, keep_ref, step_ref, conv_ref, inj_ref, read_ref, rates_ref, out_ref, start_ref, state_ref):
    chunk, tiles = step_ref.shape[0], step_ref.shape[1] // LANES
    at = pl.program_id(0)
    @pl.when(at % per_block == 0)
    def _():
        state_ref[...] = state_ref[...] * keep_ref[at // per_block]
    @pl.when(at == 0)
    def _():
        state_ref[...] = jnp.zeros_like(state_ref)
    start_ref[0] = state_ref[...]
    rates = [rates_ref[:, k*LANES:(k+1)*LANES] for k in range(tiles)]
    def group(g, state):
        base = pl.multiple_of(g * 8, 8)
        state = list(state)
        steps = [step_ref[pl.ds(base, 8), k*LANES:(k+1)*LANES] for k in range(tiles)]
        pushes = [steps[k] * conv_ref[pl.ds(base, 8), k*LANES:(k+1)*LANES] for k in range(tiles)]
        parts = [[] for _ in range(tiles)]
        for i in range(8):
            inject, read = inj_ref[base + i], read_ref[base + i]
            for k in range(tiles):
                decay = jnp.exp(steps[k][i:i+1] * rates[k])
                state[k] = decay * state[k] + pushes[k][i:i+1] * inject
                parts[k].append(fold(state[k] * read))
        for k in range(tiles):
            out_ref[pl.ds(base, 8), k*LANES:(k+1)*LANES] = row_sums(parts[k])
        return tuple(state)
    state = tuple(state_ref[:, k*LANES:(k+1)*LANES] for k in range(tiles))
    state = lax.fori_loop(0, chunk // 8, group, state)
    for k in range(tiles):
        state_ref[:, k*LANES:(k+1)*LANES] = state[k]

def scan_forward(keep, step, conv, inject, read, rates, chunk, block):
    rows, width = step.shape
    grid = rows // chunk
    row_spec = pl.BlockSpec((chunk, width), lambda i, *_: (i, 0))
    wide_spec = pl.BlockSpec((chunk, STATE, LANES), lambda i, *_: (i, 0, 0))
    return pl.pallas_call(
        functools.partial(scan_kernel, block // chunk),
        grid_spec=pltpu.PrefetchScalarGridSpec(num_scalar_prefetch=1, grid=(grid,),
            in_specs=[row_spec, row_spec, wide_spec, wide_spec, pl.BlockSpec((STATE, width), lambda i, *_: (0, 0))],
            out_specs=[row_spec, pl.BlockSpec((1, STATE, width), lambda i, *_: (i, 0, 0))],
            scratch_shapes=[pltpu.VMEM((STATE, width), jnp.float32)]),
        out_shape=[jax.ShapeDtypeStruct((rows, width), jnp.float32), jax.ShapeDtypeStruct((grid, STATE, width), jnp.float32)],
        compiler_params=pltpu.CompilerParams(vmem_limit_bytes=40<<20),
        name="state_scan",
    )(keep, step, conv, inject, read, rates)

def back_kernel(per_block, keep_ref, step_ref, conv_ref, inj_ref, read_ref, rates_ref, grad_ref, start_ref,
                gstep_ref, gconv_ref, ginj_ref, gread_ref, grate_ref, later_ref, hist_ref, decay_ref):
    chunk, tiles = step_ref.shape[0], step_ref.shape[1] // LANES
    at = pl.num_programs(0) - 1 - pl.program_id(0)
    lanes = [slice(k*LANES, (k+1)*LANES) for k in range(tiles)]
    @pl.when(pl.program_id(0) == 0)
    def _():
        later_ref[...] = jnp.zeros_like(later_ref)
        grate_ref[...] = jnp.zeros_like(grate_ref)
    def forward(g, state):
        base = pl.multiple_of(g * 8, 8)
        state = list(state)
        steps = [step_ref[pl.ds(base, 8), lanes[k]] for k in range(tiles)]
        pushes = [steps[k] * conv_ref[pl.ds(base, 8), lanes[k]] for k in range(tiles)]
        for i in range(8):
            inject = inj_ref[base + i]
            for k in range(tiles):
                decay = jnp.exp(steps[k][i:i+1] * rates_ref[:, lanes[k]])
                decay_ref[base + i, :, lanes[k]] = decay
                hist_ref[base + i, :, lanes[k]] = state[k]
                state[k] = decay * state[k] + pushes[k][i:i+1] * inject
        return tuple(state)
    state = lax.fori_loop(0, chunk // 8, forward, tuple(start_ref[0, :, lanes[k]] for k in range(tiles)))
    for k in range(tiles):
        hist_ref[chunk, :, lanes[k]] = state[k]
    def backward(j, later):
        base = pl.multiple_of((chunk // 8 - 1 - j) * 8, 8)
        later = list(later)
        steps = [step_ref[pl.ds(base, 8), lanes[k]] for k in range(tiles)]
        convs = [conv_ref[pl.ds(base, 8), lanes[k]] for k in range(tiles)]
        grads = [grad_ref[pl.ds(base, 8), lanes[k]] for k in range(tiles)]
        pushes = [steps[k] * convs[k] for k in range(tiles)]
        pulls = [[None] * 8 for _ in range(tiles)]
        drives = [[None] * 8 for _ in range(tiles)]
        rate_sums = [None] * tiles
        for i in range(7, -1, -1):
            inject, read = inj_ref[base + i], read_ref[base + i]
            ginj = gread = None
            for k in range(tiles):
                grad = grads[k][i:i+1]
                total = read * grad + later[k]
                later[k] = decay_ref[base + i, :, lanes[k]] * total
                pull = later[k] * hist_ref[base + i, :, lanes[k]]
                term = pull * steps[k][i:i+1]
                rate_sums[k] = term if rate_sums[k] is None else rate_sums[k] + term
                pulls[k][i] = fold(pull * rates_ref[:, lanes[k]])
                drives[k][i] = fold(total * inject)
                term = total * pushes[k][i:i+1]
                ginj = term if ginj is None else ginj + term
                term = hist_ref[base + i + 1, :, lanes[k]] * grad
                gread = term if gread is None else gread + term
            ginj_ref[base + i] = ginj
            gread_ref[base + i] = gread
        for k in range(tiles):
            grate_ref[:, lanes[k]] += rate_sums[k]
            drive = row_sums(drives[k])
            gstep_ref[pl.ds(base, 8), lanes[k]] = row_sums(pulls[k]) + drive * convs[k]
            gconv_ref[pl.ds(base, 8), lanes[k]] = drive * steps[k]
        return tuple(later)
    later = lax.fori_loop(0, chunk // 8, backward, tuple(later_ref[:, lanes[k]] for k in range(tiles)))
    factor = jnp.where(at % per_block == 0, keep_ref[at // per_block], 1.0)
    for k in range(tiles):
        later_ref[:, lanes[k]] = later[k] * factor

def scan_backward(keep, step, conv, inject, read, rates, grad, starts, chunk, block):
    rows, width = step.shape
    grid = rows // chunk
    row_spec = pl.BlockSpec((chunk, width), lambda i, *_: (grid - 1 - i, 0))
    wide_spec = pl.BlockSpec((chunk, STATE, LANES), lambda i, *_: (grid - 1 - i, 0, 0))
    all_spec = pl.BlockSpec((STATE, width), lambda i, *_: (0, 0))
    return pl.pallas_call(
        functools.partial(back_kernel, block // chunk),
        grid_spec=pltpu.PrefetchScalarGridSpec(num_scalar_prefetch=1, grid=(grid,),
            in_specs=[row_spec, row_spec, wide_spec, wide_spec, all_spec, row_spec, pl.BlockSpec((1, STATE, width), lambda i, *_: (grid - 1 - i, 0, 0))],
            out_specs=[row_spec, row_spec, wide_spec, wide_spec, all_spec],
            scratch_shapes=[pltpu.VMEM((STATE, width), jnp.float32), pltpu.VMEM((chunk + 1, STATE, width), jnp.float32), pltpu.VMEM((chunk, STATE, width), jnp.float32)]),
        out_shape=[jax.ShapeDtypeStruct((rows, width), jnp.float32)] * 2 + [jax.ShapeDtypeStruct((rows, STATE, LANES), jnp.float32)] * 2 + [jax.ShapeDtypeStruct((STATE, width), jnp.float32)],
        compiler_params=pltpu.CompilerParams(vmem_limit_bytes=50<<20),
        name="state_back",
    )(keep, step, conv, inject, read, rates, grad, starts)


def adam_update(weight, gradient, first_old, second_old, step_float):
    mean_new = beta_first * first_old + (1.0 - beta_first) * gradient
    square_new = beta_second * second_old + (1.0 - beta_second) * gradient * gradient
    fix_first = 1.0 - jnp.power(beta_first, step_float)
    fix_second = 1.0 - jnp.power(beta_second, step_float)
    delta_new = -learn_rate * (
        mean_new / fix_first / (jnp.sqrt(square_new / fix_second) + adam_floor)
        + weight_decay * weight.astype(jnp.float32)
    )
    return (mean_new, square_new, delta_new)


def layout(lengths, buffer_rows):
    index = jnp.arange(lengths.shape[0], dtype=jnp.int32)
    count_blocks = (lengths + (BLOCK - 1)) // BLOCK
    earlier = (index[None, :] < index[:, None]).astype(jnp.int32)
    first_block = jnp.sum(earlier * count_blocks[None, :], axis=1)
    places = jnp.arange(buffer_rows, dtype=jnp.int32)
    owner = (
        jnp.sum((first_block[None, :] <= (places // BLOCK)[:, None]).astype(jnp.int32), axis=1) - 1
    )
    pick = (owner[:, None] == index[None, :]).astype(jnp.int32)
    seq_length = jnp.sum(pick * lengths[None, :], axis=1)
    offset = places - BLOCK * jnp.sum(pick * first_block[None, :], axis=1)
    live = offset < seq_length
    begins = live & (offset == 0)
    return (owner, offset, live, begins)


def trade(pieces):
    return lax.all_to_all(pieces, "dp", 0, 0)


def spread(rows, groups):
    got = trade(jnp.broadcast_to(rows[None], (groups,) + rows.shape))
    return got.reshape((groups * rows.shape[0],) + rows.shape[1:])


def collect(partial, groups, kind=jnp.bfloat16):
    pieces = partial.astype(kind).reshape((groups, partial.shape[0] // groups) + partial.shape[1:])
    return jnp.sum(trade(pieces).astype(jnp.float32), axis=0)


def padded_part(part, ranks):
    unit = max(8, LANES // ranks)
    return -(-part // unit) * unit


def deal_columns(shard, groups, part, wide_part):
    rows, width = shard.shape
    runs = width // (groups * part)
    pieces = shard.reshape(rows, runs, groups, part).transpose(2, 0, 1, 3)
    got = trade(pieces.reshape(groups, rows, runs * part)).transpose(1, 0, 2)
    got = jnp.pad(got.reshape(rows, groups * runs, part), ((0, 0), (0, 0), (0, wide_part - part)))
    return got.reshape(rows, groups * runs * wide_part)


def return_columns(dealt, groups, part, wide_part):
    rows, width = dealt.shape
    runs = width // (groups * wide_part)
    pieces = dealt.reshape(rows, groups * runs, wide_part)[:, :, :part]
    got = trade(pieces.reshape(rows, groups, runs * part).transpose(1, 0, 2))
    return got.reshape(groups, rows, runs, part).transpose(1, 2, 0, 3).reshape(rows, -1)


def deal_rows(shard, groups, wide_part):
    rows, width = shard.shape
    part = rows // groups
    got = trade(shard.reshape(groups, part, width))
    got = got.transpose(1, 0, 2).reshape(part, groups * width)
    return jnp.pad(got, ((0, wide_part - part), (0, 0)))


def return_rows(dealt, groups, part):
    width = dealt.shape[1]
    got = trade(dealt[:part].reshape(part, groups, width // groups).transpose(1, 0, 2))
    return got.reshape(groups * part, width // groups)


def whole(shard):
    return lax.all_gather(shard, "shard", axis=0, tiled=True)


def owned_sum(partial):
    return lax.psum_scatter(partial, "shard", scatter_dimension=0, tiled=True)


def lane_copies(values):
    return jnp.broadcast_to(values[:, :, None], values.shape + (LANES,))


def shards(
    groups,
    ranks,
    tokens,
    cotangent,
    lengths,
    step_count,
    norm_gains,
    qkv_weight,
    attn_weight,
    mixer_in,
    mixer_table,
    mixer_out,
    ffn_in,
    ffn_out,
    first_gains,
    first_qkv,
    first_attn,
    first_mixin,
    first_table,
    first_mixout,
    first_ffnin,
    first_ffnout,
    second_gains,
    second_qkv,
    second_attn,
    second_mixin,
    second_table,
    second_mixout,
    second_ffnin,
    second_ffnout,
):
    low = jnp.bfloat16
    buffer_rows = tokens.shape[0]
    model_width = tokens.shape[1]
    here = lax.axis_index("dp")
    part_inner = INNER // groups // ranks
    part_hidden = FF // groups // ranks
    wide_inner = padded_part(part_inner, ranks)
    wide_hidden = padded_part(part_hidden, ranks)
    inner = wide_inner * ranks
    hidden_units = wide_hidden * ranks
    part_model = model_width // ranks
    table_width = mixer_table.shape[1]
    gain_count = norm_gains.shape[1]

    table_part = lax.dynamic_slice_in_dim(mixer_table, here * part_inner, part_inner, axis=0)
    table_part = jnp.pad(table_part, ((0, 0), (0, 2 * LANES - table_width)))
    fold_rows = part_inner * 2 * LANES // part_model
    first_pack = jnp.concatenate(
        [qkv_weight, table_part.reshape(part_model, fold_rows), norm_gains], axis=1
    )
    first_full = whole(first_pack)
    weight_in = whole(deal_columns(mixer_in, groups, part_inner, wide_inner))
    weight_mix = whole(deal_rows(mixer_out, groups, wide_inner))
    weight_attn = whole(spread(attn_weight, groups).reshape(groups, part_model, -1).transpose(1, 0, 2).reshape(part_model, model_width))
    weight_up = whole(deal_columns(ffn_in, groups, part_hidden, wide_hidden))
    weight_down = whole(deal_rows(ffn_out, groups, wide_hidden))

    qkv_width = qkv_weight.shape[1]
    weight_qkv = first_full[:, :qkv_width]
    table_low = first_full[:, qkv_width : qkv_width + fold_rows].reshape(
        ranks, part_inner, 2 * LANES
    )
    table_low = jnp.pad(
        table_low[:, :, :table_width], ((0, 0), (0, wide_inner - part_inner), (0, 0))
    ).reshape(inner, table_width)
    gain_cols = first_full[:, qkv_width + fold_rows :].astype(jnp.float32)

    lengths_all = lax.all_gather(lengths, "dp", axis=0, tiled=True)
    owner, offset, live, _ = layout(lengths[0], buffer_rows)
    live_rows = live.astype(jnp.float32)
    places = jnp.arange(buffer_rows, dtype=jnp.int32)
    allowed = (owner[:, None] == owner[None, :]) & (places[None, :] <= places[:, None]) & live[
        None, :
    ] | (places[:, None] == places[None, :])
    _, offset_all, _, begins_all = jax.vmap(lambda row: layout(row, buffer_rows))(lengths_all)
    offset_all = offset_all.reshape(-1)
    block_starts = begins_all[:, ::BLOCK] | (jnp.arange(buffer_rows // BLOCK) == 0)[None, :]
    block_keep = 1.0 - block_starts.reshape(-1).astype(jnp.float32)

    inputs = tokens.astype(jnp.float32)
    scale_in = rms_scale(inputs)
    normed = (inputs * scale_in * gain_cols[:, 0]).astype(low)
    normed_all = spread(normed, groups)
    grad_out = cotangent.astype(jnp.float32) * live_rows[:, None]
    grad_ffn_all = spread(grad_out.astype(low), groups)

    heads_part = product(normed_all, weight_qkv).astype(low)
    heads_low = (
        trade(heads_part.reshape(groups, buffer_rows, qkv_width))
        .transpose(1, 0, 2)
        .reshape(buffer_rows, groups * qkv_width)
    )
    kv_width = KV * HEAD
    query = heads_low[:, :model_width].reshape(buffer_rows, KV, GROUP, HEAD)
    key_rows = heads_low[:, model_width : model_width + kv_width].reshape(buffer_rows, KV, HEAD)
    value_rows = heads_low[:, model_width + kv_width :].reshape(buffer_rows, KV, HEAD)
    factor = HEAD ** (-0.5)

    def masked_scores():
        raw_scores = (
            jnp.einsum("qkgd,skd->kgqs", query, key_rows, preferred_element_type=jnp.float32)
            * factor
        )
        return jnp.where(allowed, raw_scores, masked_score)

    scores = masked_scores()
    top_score = jnp.max(scores, axis=-1, keepdims=True)
    log_total = top_score + jnp.log(jnp.sum(jnp.exp(scores - top_score), axis=-1, keepdims=True))
    probs_low = jnp.exp(scores - log_total).astype(low)
    context = (
        jnp.einsum("kgqs,skd->qkgd", probs_low, value_rows, preferred_element_type=jnp.float32)
        .reshape(buffer_rows, model_width)
        .astype(low)
    )
    attn_raw = product(context, weight_attn)
    scale_attn = rms_scale(attn_raw)

    mixed = product(normed_all, weight_in)
    xin = mixed[:, :inner]
    gate_z = mixed[:, inner:]
    table = table_low.astype(jnp.float32)
    tap_masks = [(offset_all >= lag).astype(jnp.float32)[:, None] for lag in range(CONV)]
    taps = [shift_rows(xin, lag) * tap_masks[lag] for lag in range(CONV)]
    conv_pre = table[:, CONV]
    for lag in range(CONV):
        conv_pre = conv_pre + table[:, lag] * taps[lag]
    conv_low = silu_act(conv_pre).astype(low)
    conv_out = conv_low.astype(jnp.float32)
    proj_start = CONV + 3 + STATE
    input_proj = table_low[:, proj_start : proj_start + RANK + 2 * STATE]
    step_proj = table_low[:, proj_start + RANK + 2 * STATE :]
    double = spread(
        collect(product(conv_low, input_proj), groups, jnp.float32), groups
    )
    rank_part = double[:, :RANK].astype(low)
    inject = lane_copies(double[:, RANK : RANK + STATE])
    readout = lane_copies(double[:, RANK + STATE :])
    dt_pre = product_nt(rank_part, step_proj) + table[:, CONV + 1]
    step_size = jnp.log1p(jnp.exp(dt_pre))
    rates = -jnp.exp(table[:, CONV + 3 : CONV + 3 + STATE]).T
    states_out, chunk_starts = scan_forward(
        block_keep, step_size, conv_out, inject, readout, rates, CHUNK, BLOCK
    )
    skip_weight = table[:, CONV + 2]
    scanned = states_out + skip_weight * conv_out
    silu_z = silu_act(gate_z)
    gated_low = (scanned * silu_z).astype(low)
    mamba_raw = collect(product(gated_low, weight_mix), groups)
    scale_mamba = rms_scale(mamba_raw)
    hidden = inputs + 0.5 * (
        attn_raw * scale_attn * gain_cols[:, 1] + mamba_raw * scale_mamba * gain_cols[:, 2]
    )
    scale_hidden = rms_scale(hidden)
    normed_two = (hidden * scale_hidden * gain_cols[:, 3]).astype(low)

    normed_two_all = spread(normed_two, groups)
    both = product(normed_two_all, weight_up)
    gate_ffn = both[:, :hidden_units]
    up_ffn = both[:, hidden_units:]
    act_low = (silu_act(gate_ffn) * up_ffn).astype(low)
    ffn_raw = collect(product(act_low, weight_down), groups)
    output = (live_rows[:, None] * (hidden + ffn_raw)).astype(low)
    grad_down_w = product_tn(act_low, grad_ffn_all).astype(low)
    grad_act = product_nt(grad_ffn_all, weight_down)
    gate_sig = sigmoid(gate_ffn)
    grad_gate = grad_act * up_ffn * gate_sig * (1.0 + gate_ffn * (1.0 - gate_sig))
    grad_up = grad_act * silu_act(gate_ffn)
    grad_both = jnp.concatenate([grad_gate, grad_up], axis=1).astype(low)
    grad_up_w = product_tn(normed_two_all, grad_both).astype(low)
    grad_second = collect(product_nt(grad_both, weight_up), groups)
    back_hidden, gain_three = rms_back(hidden, scale_hidden, gain_cols[:, 3], grad_second)
    grad_hidden = grad_out + back_hidden
    ffn_done = (
        return_columns(owned_sum(grad_up_w), groups, part_hidden, wide_hidden),
        return_rows(owned_sum(grad_down_w), groups, part_hidden),
    )

    half_grad = 0.5 * grad_hidden
    grad_mamba_full, gain_two = rms_back(mamba_raw, scale_mamba, gain_cols[:, 2], half_grad)
    grad_mamba_all = spread(grad_mamba_full.astype(low), groups)
    grad_attn_full, gain_one = rms_back(attn_raw, scale_attn, gain_cols[:, 1], half_grad)
    grad_attn_low = grad_attn_full.astype(low)
    grad_attn_w = product_tn(context, grad_attn_low).astype(low)
    grad_attn_own = owned_sum(grad_attn_w)
    grad_attn_done = collect(
        grad_attn_own.reshape(part_model, groups, -1).transpose(1, 0, 2).reshape(groups * part_model, -1),
        groups,
    )
    grad_context = (
        product_nt(grad_attn_low, weight_attn).astype(low).reshape(buffer_rows, KV, GROUP, HEAD)
    )
    probs_again = jnp.exp(masked_scores() - log_total)
    grad_probs = jnp.einsum(
        "qkgd,skd->kgqs", grad_context, value_rows, preferred_element_type=jnp.float32
    )
    grad_values = jnp.einsum(
        "kgqs,qkgd->skd",
        probs_again.astype(low),
        grad_context,
        preferred_element_type=jnp.float32,
    )
    grad_scores = (
        probs_again * (grad_probs - jnp.sum(probs_again * grad_probs, axis=-1, keepdims=True))
    ).astype(low)
    grad_query = (
        jnp.einsum("kgqs,skd->qkgd", grad_scores, key_rows, preferred_element_type=jnp.float32)
        * factor
    )
    grad_keys = (
        jnp.einsum("kgqs,qkgd->skd", grad_scores, query, preferred_element_type=jnp.float32)
        * factor
    )
    grad_heads = jnp.concatenate(
        [
            grad_query.reshape(buffer_rows, model_width),
            grad_keys.reshape(buffer_rows, kv_width),
            grad_values.reshape(buffer_rows, kv_width),
        ],
        axis=1,
    ).astype(low)
    grad_heads_part = trade(
        grad_heads.reshape(buffer_rows, groups, qkv_width).transpose(1, 0, 2)
    ).reshape(groups * buffer_rows, qkv_width)
    grad_qkv_w = product_tn(normed_all, grad_heads_part).astype(low)

    grad_mix_w = product_tn(gated_low, grad_mamba_all).astype(low)
    grad_mix_done = return_rows(owned_sum(grad_mix_w), groups, part_inner)
    grad_gated = product_nt(grad_mamba_all, weight_mix)
    grad_scanned = grad_gated * silu_z
    grad_gate_z = grad_gated * scanned * silu_slope(gate_z)
    grad_skip = jnp.sum(grad_scanned * conv_out, axis=0)
    grad_step, grad_conv_scan, grad_inject, grad_readout, grad_rates = scan_backward(
        block_keep,
        step_size,
        conv_out,
        inject,
        readout,
        rates,
        grad_scanned,
        chunk_starts,
        CHUNK,
        BLOCK,
    )
    grad_pre = grad_step * sigmoid(dt_pre)
    grad_step_bias = jnp.sum(grad_pre, axis=0)
    grad_pre_low = grad_pre.astype(low)
    grad_step_proj = product_tn(grad_pre_low, rank_part)
    grad_rank = product(grad_pre_low, step_proj)
    grad_double = spread(
        collect(
            jnp.concatenate(
                [grad_rank, jnp.sum(grad_inject, axis=2), jnp.sum(grad_readout, axis=2)], axis=1
            ),
            groups,
            jnp.float32,
        ).astype(low),
        groups,
    )
    grad_input_proj = product_tn(conv_low, grad_double)
    grad_conv_out = (
        product_nt(grad_double, input_proj) + grad_conv_scan + skip_weight * grad_scanned
    )
    grad_conv = grad_conv_out * silu_slope(conv_pre)
    grad_conv_bias = jnp.sum(grad_conv, axis=0)
    grad_taps = jnp.stack([jnp.sum(grad_conv * taps[lag], axis=0) for lag in range(CONV)], axis=1)
    grad_xin = unshift_rows(grad_conv * tap_masks[0] * table[:, 0], 0)
    for lag in range(1, CONV):
        grad_xin = grad_xin + unshift_rows(grad_conv * tap_masks[lag] * table[:, lag], lag)
    grad_mixed = jnp.concatenate([grad_xin, grad_gate_z], axis=1).astype(low)
    grad_in_w = product_tn(normed_all, grad_mixed).astype(low)
    grad_normed = collect(
        product_nt(grad_heads_part, weight_qkv) + product_nt(grad_mixed, weight_in), groups
    )
    grad_log_rates = (grad_rates * rates).T
    grad_table = jnp.concatenate(
        [
            grad_taps,
            grad_conv_bias[:, None],
            grad_step_bias[:, None],
            grad_skip[:, None],
            grad_log_rates,
            grad_input_proj,
            grad_step_proj,
        ],
        axis=1,
    ).reshape(ranks, wide_inner, table_width)[:, :part_inner]
    back_inputs, gain_zero = rms_back(inputs, scale_in, gain_cols[:, 0], grad_normed)
    grad_tokens = grad_hidden + back_inputs
    grad_gains = jnp.stack([gain_zero, gain_one, gain_two, gain_three], axis=1)

    grad_qkv_done = owned_sum(grad_qkv_w).astype(jnp.float32)
    grad_in_done = return_columns(owned_sum(grad_in_w), groups, part_inner, wide_inner)
    small = jnp.concatenate(
        [
            jnp.pad(grad_table, ((0, 0), (0, 0), (0, 2 * LANES - table_width))).reshape(
                model_width, fold_rows
            ),
            grad_gains,
        ],
        axis=1,
    )
    small_all = spread(owned_sum(small), groups).reshape(groups, part_model, fold_rows + gain_count)
    grad_table_done = small_all[:, :, :fold_rows].reshape(groups * part_inner, 2 * LANES)[
        :, :table_width
    ]
    grad_gains_done = jnp.sum(small_all[:, :, fold_rows:], axis=0)

    owned = (norm_gains, qkv_weight, attn_weight, mixer_in, mixer_table, mixer_out, ffn_in, ffn_out)
    grads_owned = (
        grad_gains_done,
        grad_qkv_done,
        grad_attn_done,
        grad_in_done.astype(jnp.float32),
        grad_table_done,
        grad_mix_done.astype(jnp.float32),
        ffn_done[0].astype(jnp.float32),
        ffn_done[1].astype(jnp.float32),
    )
    firsts = (
        first_gains,
        first_qkv,
        first_attn,
        first_mixin,
        first_table,
        first_mixout,
        first_ffnin,
        first_ffnout,
    )
    seconds = (
        second_gains,
        second_qkv,
        second_attn,
        second_mixin,
        second_table,
        second_mixout,
        second_ffnin,
        second_ffnout,
    )
    step_float = step_count[0].astype(jnp.float32)
    updates = [
        adam_update(owned[slot], grads_owned[slot], firsts[slot], seconds[slot], step_float)
        for slot in range(8)
    ]
    means = tuple((entry[0] for entry in updates))
    squares = tuple((entry[1] for entry in updates))
    deltas = tuple((entry[2] for entry in updates))
    return (output, grad_tokens) + grads_owned + means + squares + deltas


def solution(mesh):
    in_specs = (
        P(("dp", "shard"), None),
        P(("dp", "shard"), None),
        P(("dp", "shard"), None),
        P(),
        P("shard", None),
        P("shard", "dp"),
        P("shard", "dp"),
        P("shard", "dp"),
        P("shard", None),
        P("shard", "dp"),
        P("shard", "dp"),
        P("shard", "dp"),
        P("shard", None),
        P("shard", "dp"),
        P("shard", "dp"),
        P("shard", "dp"),
        P("shard", None),
        P("shard", "dp"),
        P("shard", "dp"),
        P("shard", "dp"),
        P("shard", None),
        P("shard", "dp"),
        P("shard", "dp"),
        P("shard", "dp"),
        P("shard", None),
        P("shard", "dp"),
        P("shard", "dp"),
        P("shard", "dp"),
    )
    out_specs = (
        P(("dp", "shard"), None),
        P(("dp", "shard"), None),
        P("shard", None),
        P("shard", "dp"),
        P("shard", "dp"),
        P("shard", "dp"),
        P("shard", None),
        P("shard", "dp"),
        P("shard", "dp"),
        P("shard", "dp"),
        P("shard", None),
        P("shard", "dp"),
        P("shard", "dp"),
        P("shard", "dp"),
        P("shard", None),
        P("shard", "dp"),
        P("shard", "dp"),
        P("shard", "dp"),
        P("shard", None),
        P("shard", "dp"),
        P("shard", "dp"),
        P("shard", "dp"),
        P("shard", None),
        P("shard", "dp"),
        P("shard", "dp"),
        P("shard", "dp"),
        P("shard", None),
        P("shard", "dp"),
        P("shard", "dp"),
        P("shard", "dp"),
        P("shard", None),
        P("shard", "dp"),
        P("shard", "dp"),
        P("shard", "dp"),
    )
    return jax.shard_map(functools.partial(shards, mesh.shape["dp"], mesh.shape["shard"]), mesh=mesh, in_specs=in_specs, out_specs=out_specs, check_vma=False)
```

```python
import functools

import jax
import jax.numpy as jnp
from jax import lax
from jax.experimental import pallas as pl
from jax.experimental.pallas import tpu as pltpu
from jax.sharding import PartitionSpec as P

KV = 5
HEAD = 64
GROUP = 5
INNER = 3200
STATE = 16
CONV = 4
RANK = 100
FF = 5504
BLOCK = 128
LANES = 128


epsilon = 1e-06
beta_first = 0.9
beta_second = 0.95
adam_floor = 1e-08
learn_rate = 0.01
weight_decay = 0.1
masked_score = -1e30


def product(left, right):
    return jnp.dot(left, right, preferred_element_type=jnp.float32)


def product_tn(left, right):
    return lax.dot_general(
        left, right, (((0,), (0,)), ((), ())), preferred_element_type=jnp.float32
    )


def product_nt(left, right):
    return lax.dot_general(
        left, right, (((1,), (1,)), ((), ())), preferred_element_type=jnp.float32
    )


def sigmoid(values):
    return 1.0 / (1.0 + jnp.exp(-values))


def silu_act(values):
    return values / (1.0 + jnp.exp(-values))


def silu_slope(values):
    gate_sig = sigmoid(values)
    return gate_sig * (1.0 + values * (1.0 - gate_sig))


def rms_scale(values):
    return lax.rsqrt(jnp.mean(values * values, axis=-1, keepdims=True) + epsilon)


def rms_back(values, scale, gain, incoming):
    weighted = incoming * gain
    inner_mean = jnp.mean(weighted * values, axis=-1, keepdims=True)
    return (
        scale * weighted - values * (scale * scale * scale) * inner_mean,
        jnp.sum(incoming * values * scale, axis=0),
    )


def shift_rows(values, lag):
    if lag == 0:
        return values
    return jnp.concatenate(
        [jnp.zeros((lag, values.shape[1]), values.dtype), values[: values.shape[0] - lag]], axis=0
    )


def unshift_rows(values, lag):
    if lag == 0:
        return values
    return jnp.concatenate([values[lag:], jnp.zeros((lag, values.shape[1]), values.dtype)], axis=0)


def row_sums(parts):
    rows = lax.broadcasted_iota(jnp.int32, (8, LANES), 0)
    quads = []
    low = rows < 4
    for i in range(4):
        a, b = parts[i], parts[i + 4]
        quads.append(jnp.where(low, a, b) + pltpu.roll(jnp.where(low, b, a), 4, 0))
    pairs = []
    low = (rows & 3) < 2
    for i in range(2):
        a, b = quads[i], quads[i + 2]
        pairs.append(jnp.where(low, a + pltpu.roll(a, 6, 0), b + pltpu.roll(b, 2, 0)))
    a, b = pairs
    return jnp.where((rows & 1) < 1, a + pltpu.roll(a, 7, 0), b + pltpu.roll(b, 1, 0))


def fold_rows_in(values):
    return values[:8] + values[8:]


def lane_tiles(width):
    return [slice(k * LANES, (k + 1) * LANES) for k in range(width // LANES)]


def scan_kernel(
    keep_ref,
    step_ref,
    conv_ref,
    inject_ref,
    read_ref,
    rates_ref,
    out_ref,
    start_ref,
    inject_wide_ref,
    read_wide_ref,
    state_ref,
):
    at = pl.program_id(0)
    tiles = lane_tiles(step_ref.shape[1])

    @pl.when(at == 0)
    def _():
        state_ref[...] = jnp.zeros_like(state_ref)

    state_ref[...] = state_ref[...] * keep_ref[at]
    start_ref[0] = state_ref[...]
    rates = [rates_ref[:, tile] for tile in tiles]

    def group(turn, state):
        base = pl.multiple_of(turn * 8, 8)
        state = list(state)
        steps = [step_ref[pl.ds(base, 8), tile] for tile in tiles]
        pushes = [
            steps[k] * conv_ref[pl.ds(base, 8), tile] for k, tile in enumerate(tiles)
        ]
        parts = [[] for _ in tiles]
        turned = [pltpu.roll(ref[...], BLOCK - base, 1) for ref in (inject_ref, read_ref)]
        for i in range(8):
            inject, read = [
                jnp.broadcast_to(values[:, i : i + 1], (STATE, LANES)) for values in turned
            ]
            inject_wide_ref[base + i], read_wide_ref[base + i] = inject, read
            for k in range(len(tiles)):
                decay = jnp.exp(steps[k][i : i + 1] * rates[k])
                state[k] = decay * state[k] + pushes[k][i : i + 1] * inject
                parts[k].append(fold_rows_in(state[k] * read))
        for k, tile in enumerate(tiles):
            out_ref[pl.ds(base, 8), tile] = row_sums(parts[k])
        return tuple(state)

    state = lax.fori_loop(0, BLOCK // 8, group, tuple(state_ref[:, tile] for tile in tiles))
    for k, tile in enumerate(tiles):
        state_ref[:, tile] = state[k]


def scan_forward(keep, step, conv, inject, read, rates):
    rows, width = step.shape
    blocks = rows // BLOCK
    row_spec = pl.BlockSpec((BLOCK, width), lambda i, *_: (i, 0))
    state_spec = pl.BlockSpec((STATE, BLOCK), lambda i, *_: (0, i))
    wide_spec = pl.BlockSpec((BLOCK, STATE, LANES), lambda i, *_: (i, 0, 0))
    return pl.pallas_call(
        scan_kernel,
        grid_spec=pltpu.PrefetchScalarGridSpec(
            num_scalar_prefetch=1,
            grid=(blocks,),
            in_specs=[
                row_spec,
                row_spec,
                state_spec,
                state_spec,
                pl.BlockSpec((STATE, width), lambda i, *_: (0, 0)),
            ],
            out_specs=[
                row_spec,
                pl.BlockSpec((1, STATE, width), lambda i, *_: (i, 0, 0)),
                wide_spec,
                wide_spec,
            ],
            scratch_shapes=[pltpu.VMEM((STATE, width), jnp.float32)],
        ),
        out_shape=[
            jax.ShapeDtypeStruct((rows, width), jnp.float32),
            jax.ShapeDtypeStruct((blocks, STATE, width), jnp.float32),
        ]
        + [jax.ShapeDtypeStruct((rows, STATE, LANES), jnp.float32)] * 2,
        cost_estimate=pl.CostEstimate(
            flops=30 * rows * STATE * width,
            bytes_accessed=140 * rows * width,
            transcendentals=rows * STATE * width,
        ),
        compiler_params=pltpu.CompilerParams(vmem_limit_bytes=24 * 2**20),
        name="state_scan",
    )(keep, step, conv, inject, read, rates)


def back_kernel(
    keep_ref,
    step_ref,
    conv_ref,
    inject_ref,
    read_ref,
    rates_ref,
    grad_ref,
    start_ref,
    gstep_ref,
    gconv_ref,
    ginject_ref,
    gread_ref,
    grate_ref,
    later_ref,
    history_ref,
    decay_ref,
    sums_ref,
):
    tiles = lane_tiles(step_ref.shape[1])
    at = pl.num_programs(0) - 1 - pl.program_id(0)

    @pl.when(pl.program_id(0) == 0)
    def _():
        later_ref[...] = jnp.zeros_like(later_ref)
        grate_ref[...] = jnp.zeros_like(grate_ref)

    def forward(turn, state):
        base = pl.multiple_of(turn * 8, 8)
        state = list(state)
        steps = [step_ref[pl.ds(base, 8), tile] for tile in tiles]
        pushes = [
            steps[k] * conv_ref[pl.ds(base, 8), tile] for k, tile in enumerate(tiles)
        ]
        for i in range(8):
            inject = inject_ref[base + i]
            for k, tile in enumerate(tiles):
                decay = jnp.exp(steps[k][i : i + 1] * rates_ref[:, tile])
                decay_ref[base + i, :, tile] = decay
                history_ref[base + i, :, tile] = state[k]
                state[k] = decay * state[k] + pushes[k][i : i + 1] * inject
        return tuple(state)

    state = lax.fori_loop(
        0, BLOCK // 8, forward, tuple(start_ref[0, :, tile] for tile in tiles)
    )
    for k, tile in enumerate(tiles):
        history_ref[BLOCK, :, tile] = state[k]

    def backward(turn, later):
        base = pl.multiple_of((BLOCK // 8 - 1 - turn) * 8, 8)
        later = list(later)
        steps = [step_ref[pl.ds(base, 8), tile] for tile in tiles]
        convs = [conv_ref[pl.ds(base, 8), tile] for tile in tiles]
        grads = [grad_ref[pl.ds(base, 8), tile] for tile in tiles]
        pushes = [steps[k] * convs[k] for k in range(len(tiles))]
        pulls = [[None] * 8 for _ in tiles]
        drives = [[None] * 8 for _ in tiles]
        rate_sums = [None for _ in tiles]
        for i in range(7, -1, -1):
            sums = [None, None]
            inject, read = inject_ref[base + i], read_ref[base + i]
            for k, tile in enumerate(tiles):
                grad = grads[k][i : i + 1]
                total = read * grad + later[k]
                later[k] = decay_ref[base + i, :, tile] * total
                pull = later[k] * history_ref[base + i, :, tile]
                pulls[k][i] = fold_rows_in(pull * rates_ref[:, tile])
                drives[k][i] = fold_rows_in(total * inject)
                terms = [total * pushes[k][i : i + 1], history_ref[base + i + 1, :, tile] * grad]
                sums = [term if old is None else old + term for old, term in zip(sums, terms)]
                term = pull * steps[k][i : i + 1]
                rate_sums[k] = term if rate_sums[k] is None else rate_sums[k] + term
            sums_ref[0, base + i], sums_ref[1, base + i] = sums
        for k, tile in enumerate(tiles):
            grate_ref[:, tile] += rate_sums[k]
            drive = row_sums(drives[k])
            gstep_ref[pl.ds(base, 8), tile] = row_sums(pulls[k]) + drive * convs[k]
            gconv_ref[pl.ds(base, 8), tile] = drive * steps[k]
        return tuple(later)

    later = lax.fori_loop(
        0, BLOCK // 8, backward, tuple(later_ref[:, tile] for tile in tiles)
    )
    ones = jnp.ones((LANES, LANES), jnp.bfloat16)
    lane = lax.broadcasted_iota(jnp.int32, (STATE, BLOCK), 1)
    ginject_ref[...] = jnp.zeros_like(ginject_ref)
    gread_ref[...] = jnp.zeros_like(gread_ref)

    def lane_sums(turn, none):
        base = pl.multiple_of(turn * 32, 32)
        for which, ref in enumerate((ginject_ref, gread_ref)):
            values = sums_ref[which, pl.ds(base, 32)].reshape(32 * STATE, LANES)
            high = values.astype(jnp.bfloat16)
            rest = (values - high.astype(jnp.float32)).astype(jnp.bfloat16)
            totals = jnp.dot(high, ones, preferred_element_type=jnp.float32) + jnp.dot(
                rest, ones, preferred_element_type=jnp.float32
            )
            kept = ref[...]
            for i in range(32):
                kept = jnp.where(lane == base + i, totals[i * STATE : (i + 1) * STATE], kept)
            ref[...] = kept
        return none

    lax.fori_loop(0, BLOCK // 32, lane_sums, 0)
    for k, tile in enumerate(tiles):
        later_ref[:, tile] = later[k] * keep_ref[at]


def scan_backward(keep, step, conv, inject, read, rates, grad, starts):
    rows, width = step.shape
    blocks = rows // BLOCK
    row_spec = pl.BlockSpec((BLOCK, width), lambda i, *_: (blocks - 1 - i, 0))
    wide_spec = pl.BlockSpec((BLOCK, STATE, LANES), lambda i, *_: (blocks - 1 - i, 0, 0))
    all_spec = pl.BlockSpec((STATE, width), lambda i, *_: (0, 0))
    flat_spec = pl.BlockSpec((STATE, BLOCK), lambda i, *_: (0, blocks - 1 - i))
    return pl.pallas_call(
        back_kernel,
        grid_spec=pltpu.PrefetchScalarGridSpec(
            num_scalar_prefetch=1,
            grid=(blocks,),
            in_specs=[
                row_spec,
                row_spec,
                wide_spec,
                wide_spec,
                all_spec,
                row_spec,
                pl.BlockSpec((1, STATE, width), lambda i, *_: (blocks - 1 - i, 0, 0)),
            ],
            out_specs=[row_spec, row_spec, flat_spec, flat_spec, all_spec],
            scratch_shapes=[
                pltpu.VMEM((STATE, width), jnp.float32),
                pltpu.VMEM((BLOCK + 1, STATE, width), jnp.float32),
                pltpu.VMEM((BLOCK, STATE, width), jnp.float32),
                pltpu.VMEM((2, BLOCK, STATE, LANES), jnp.float32),
            ],
        ),
        out_shape=[jax.ShapeDtypeStruct((rows, width), jnp.float32)] * 2
        + [jax.ShapeDtypeStruct((STATE, rows), jnp.float32)] * 2
        + [jax.ShapeDtypeStruct((STATE, width), jnp.float32)],
        cost_estimate=pl.CostEstimate(
            flops=60 * rows * STATE * width,
            bytes_accessed=260 * rows * width,
            transcendentals=rows * STATE * width,
        ),
        compiler_params=pltpu.CompilerParams(vmem_limit_bytes=40 * 2**20),
        name="state_back",
    )(keep, step, conv, inject, read, rates, grad, starts)


def adam_kernel(
    fix_ref, weight_ref, grad_ref, first_ref, second_ref, out_ref, mean_ref, square_ref, delta_ref
):
    gradient = grad_ref[...].astype(jnp.float32)
    out_ref[...] = gradient
    mean_new = beta_first * first_ref[...] + (1.0 - beta_first) * gradient
    square_new = beta_second * second_ref[...] + (1.0 - beta_second) * gradient * gradient
    mean_ref[...] = mean_new
    square_ref[...] = square_new
    delta_ref[...] = -learn_rate * (
        mean_new / fix_ref[0] / (jnp.sqrt(square_new / fix_ref[1]) + adam_floor)
        + weight_decay * weight_ref[...].astype(jnp.float32)
    )


def adam_rows(weight, gradient, first_old, second_old, step_float):
    rows, width = weight.shape
    across = -(-rows // LANES) * LANES * width < -(-width // LANES) * LANES * rows
    operands = (weight, gradient, first_old, second_old)
    if across:
        operands = tuple(values.T for values in operands)
        rows, width = width, rows
    sizes = [n for n in range(8, rows, 8) if rows % n == 0 and n * width <= 2**17]
    size = max(sizes, default=rows)
    fixes = jnp.stack(
        [1.0 - jnp.power(beta_first, step_float), 1.0 - jnp.power(beta_second, step_float)]
    )
    spec = pl.BlockSpec((size, width), lambda i, *_: (i, 0))
    results = pl.pallas_call(
        adam_kernel,
        grid_spec=pltpu.PrefetchScalarGridSpec(
            num_scalar_prefetch=1, grid=(rows // size,), in_specs=[spec] * 4, out_specs=[spec] * 4
        ),
        out_shape=[jax.ShapeDtypeStruct((rows, width), jnp.float32)] * 4,
        cost_estimate=pl.CostEstimate(
            flops=20 * rows * width, bytes_accessed=28 * rows * width, transcendentals=rows * width
        ),
        compiler_params=pltpu.CompilerParams(vmem_limit_bytes=16 * 2**20),
        name="adam_rows",
    )(fixes, *operands)
    return [values.T for values in results] if across else results


def by_place(body):
    def kernel(here_ref, *refs):
        for here in range(4):
            pl.when(here_ref[0] == here)(functools.partial(body, here, *refs))

    return kernel


def column_runs(values, starts, width, padding=0):
    parts = []
    for start in starts:
        parts.append(values[:, start : start + width])
        if padding:
            parts.append(jnp.zeros((values.shape[0], padding), values.dtype))
    return jnp.concatenate(parts, axis=1)


def place_call(body, here, operands, shapes, name):
    return pl.pallas_call(
        by_place(body),
        grid_spec=pltpu.PrefetchScalarGridSpec(
            num_scalar_prefetch=1,
            in_specs=[pl.BlockSpec(memory_space=pltpu.VMEM)] * len(operands),
            out_specs=[pl.BlockSpec(memory_space=pltpu.VMEM)] * len(shapes),
        ),
        out_shape=shapes,
        compiler_params=pltpu.CompilerParams(vmem_limit_bytes=24 * 2**20),
        name=name,
    )(here, *operands)


def split_columns(shard, here, starts_of, width):
    count = len(starts_of(0)) * width

    def body(here, shard_ref, *piece_refs):
        values = shard_ref[...].astype(jnp.float32)
        for j, ref in enumerate(piece_refs):
            ref[...] = column_runs(values, starts_of(here ^ j), width).astype(ref.dtype)

    shapes = [jax.ShapeDtypeStruct((shard.shape[0], count), shard.dtype)] * 4
    return place_call(body, here, [shard], shapes, "split_columns")


def join_columns(pieces, here, width, wide):
    rows, count = pieces[0].shape
    runs = count // width

    def body(here, *refs):
        values = [ref[...].astype(jnp.float32) for ref in refs[:4]]
        refs[4][...] = jnp.concatenate(
            [
                column_runs(values[here ^ i], [r * width for r in range(runs)], width, wide - width)
                for i in range(4)
            ],
            axis=1,
        ).astype(refs[4].dtype)

    shape = jax.ShapeDtypeStruct((rows, 4 * runs * wide), pieces[0].dtype)
    return place_call(body, here, pieces, [shape], "join_columns")[0]


def split_rows(shard, here):
    part = shard.shape[0] // 4

    def body(here, shard_ref, *piece_refs):
        values = shard_ref[...].astype(jnp.float32)
        for j, ref in enumerate(piece_refs):
            i = here ^ j
            ref[...] = values[i * part : (i + 1) * part].astype(ref.dtype)

    shapes = [jax.ShapeDtypeStruct((part, shard.shape[1]), shard.dtype)] * 4
    return place_call(body, here, [shard], shapes, "split_rows")


def join_side(pieces, here, wide):
    part, width = pieces[0].shape

    def body(here, *refs):
        values = jnp.concatenate(
            [refs[here ^ i][...].astype(jnp.float32) for i in range(4)], axis=1
        )
        refs[4][:part] = values.astype(refs[4].dtype)
        if wide > part:
            refs[4][part:] = jnp.zeros((wide - part, 4 * width), refs[4].dtype)

    shape = jax.ShapeDtypeStruct((wide, 4 * width), pieces[0].dtype)
    return place_call(body, here, pieces, [shape], "join_side")[0]


def split_side(dealt, here, part):
    width = dealt.shape[1] // 4

    def body(here, dealt_ref, *piece_refs):
        values = dealt_ref[:part].astype(jnp.float32)
        for j, ref in enumerate(piece_refs):
            i = here ^ j
            ref[...] = values[:, i * width : (i + 1) * width].astype(ref.dtype)

    shapes = [jax.ShapeDtypeStruct((part, width), dealt.dtype)] * 4
    return place_call(body, here, [dealt], shapes, "split_side")


def join_rows(pieces, here):
    part, width = pieces[0].shape

    def body(here, *refs):
        refs[4][...] = jnp.concatenate(
            [refs[here ^ i][...].astype(jnp.float32) for i in range(4)], axis=0
        ).astype(refs[4].dtype)

    shape = jax.ShapeDtypeStruct((4 * part, width), pieces[0].dtype)
    return place_call(body, here, pieces, [shape], "join_rows")[0]


def join_back(pieces, here, part):
    rows, count = pieces[0].shape
    runs = count // part

    def body(here, *refs):
        values = [ref[...].astype(jnp.float32) for ref in refs[:4]]
        refs[4][...] = jnp.concatenate(
            [
                values[here ^ i][:, r * part : (r + 1) * part]
                for r in range(runs)
                for i in range(4)
            ],
            axis=1,
        ).astype(refs[4].dtype)

    shape = jax.ShapeDtypeStruct((rows, 4 * count), pieces[0].dtype)
    return place_call(body, here, pieces, [shape], "join_back")[0]


def layout(lengths, buffer_rows):
    index = jnp.arange(lengths.shape[0], dtype=jnp.int32)
    count_blocks = (lengths + (BLOCK - 1)) // BLOCK
    earlier = (index[None, :] < index[:, None]).astype(jnp.int32)
    first_block = jnp.sum(earlier * count_blocks[None, :], axis=1)
    places = jnp.arange(buffer_rows, dtype=jnp.int32)
    owner = (
        jnp.sum((first_block[None, :] <= (places // BLOCK)[:, None]).astype(jnp.int32), axis=1) - 1
    )
    pick = (owner[:, None] == index[None, :]).astype(jnp.int32)
    seq_length = jnp.sum(pick * lengths[None, :], axis=1)
    offset = places - BLOCK * jnp.sum(pick * first_block[None, :], axis=1)
    live = offset < seq_length
    begins = live & (offset == 0)
    return (owner, offset, live, begins)


def product_tt(left, right):
    return lax.dot_general(
        left, right, (((0,), (1,)), ((), ())), preferred_element_type=jnp.float32
    )


def after(values, *others):
    return lax.optimization_barrier((values, others))[0]


def swap(values, bit):
    return lax.ppermute(values, "dp", [(i, i ^ bit) for i in range(4)])


def exchange(pieces):
    if len(pieces) != 4:
        return list(lax.all_to_all(jnp.stack(pieces), "dp", 0, 0))
    return [pieces[0]] + [swap(pieces[j], j) for j in (1, 2, 3)]


def trade(pieces):
    return lax.all_to_all(pieces, "dp", 0, 0)


def spread_direct(rows, groups):
    if groups != 4:
        return list(lax.all_gather(rows, "dp", axis=0))
    return [rows] + [swap(rows, j) for j in (1, 2, 3)]


def spread(rows, groups):
    if groups != 4:
        got = lax.all_gather(rows, "dp", axis=0, tiled=True)
        return got, got
    half = rows.shape[0] // 2
    one, two = swap(rows, 1), swap(rows, 2)
    far = [swap(one[:half], 2), swap(two[half:], 1)]
    return jnp.concatenate([rows, one, two] + far, axis=0), (one, two)


def first_hop(pieces):
    if len(pieces) != 4:
        return lax.all_to_all(jnp.stack(pieces), "dp", 0, 0)
    half = pieces[0].shape[0] // 2
    return (
        swap(pieces[3][:half], 1),
        swap(pieces[3][half:], 2),
        swap(pieces[1][:half], 1),
        swap(pieces[2][half:], 2),
    )


def second_hop(pieces, hops):
    wide, kind = jnp.float32, pieces[0].dtype
    if len(pieces) != 4:
        return jnp.sum(hops.astype(wide), axis=0)
    half = pieces[0].shape[0] // 2
    one_far, two_far, one, two = hops
    top = swap((pieces[2][:half].astype(wide) + one_far.astype(wide)).astype(kind), 2)
    bottom = swap((pieces[1][half:].astype(wide) + two_far.astype(wide)).astype(kind), 1)
    own = pieces[0].astype(wide)
    return jnp.concatenate(
        [
            own[:half] + one.astype(wide) + top.astype(wide),
            own[half:] + two.astype(wide) + bottom.astype(wide),
        ],
        axis=0,
    )


def collect(pieces):
    return second_hop(pieces, first_hop(pieces))


def whole_small(values, ranks):
    if ranks != 8:
        return lax.all_gather(values, "shard", axis=1, tiled=True)
    width = values.shape[1]
    slots = jnp.zeros((values.shape[0], ranks * width), values.dtype)
    slots = lax.dynamic_update_slice_in_dim(
        slots, values, lax.axis_index("shard") * width, axis=1
    )
    for step in (1, 2, 4):
        slots = slots + lax.ppermute(slots, "shard", [(i, i ^ step) for i in range(ranks)])
    return slots


def everyone(values, groups, ranks):
    if groups != 4:
        return lax.psum(values, ("dp", "shard"))
    values = values + swap(values, 1)
    values = values + swap(values, 2)
    step = 1
    while step < ranks:
        values = values + lax.ppermute(values, "shard", [(i, i ^ step) for i in range(ranks)])
        step *= 2
    return values


def row_pieces(partial, groups):
    rows = partial.shape[0] // groups
    return [partial[j * rows : (j + 1) * rows] for j in range(groups)]


def everywhere(partial, groups):
    if groups != 4:
        return lax.psum(partial, "dp")
    rows, width = partial.shape
    part = width // 4

    def turn(values, bit):
        return jnp.concatenate(
            [values[:, (j ^ bit) * part : ((j ^ bit) + 1) * part] for j in range(4)], axis=1
        )

    half = rows // 16 * 8
    top, bottom = partial[:half], partial[half:]
    top = top + swap(turn(top, 1), 1)
    bottom = bottom + swap(turn(bottom, 2), 2)
    top = top + swap(turn(top, 2), 2)
    bottom = bottom + swap(turn(bottom, 1), 1)
    return jnp.concatenate([top, bottom], axis=0)


def padded_part(part, ranks):
    unit = max(8, LANES // ranks)
    return -(-part // unit) * unit


def deal_columns(shard, here, groups, part, wide_part):
    rows, width = shard.shape
    runs = width // (groups * part)
    if groups == 4:
        starts = lambda i: [(r * groups + i) * part for r in range(runs)]
        pieces = exchange(split_columns(shard, here, starts, part))
        return join_columns(pieces, here, part, wide_part)
    pieces = shard.reshape(rows, runs, groups, part).transpose(2, 0, 1, 3)
    got = trade(pieces.reshape(groups, rows, runs * part)).transpose(1, 0, 2)
    got = jnp.pad(got.reshape(rows, groups * runs, part), ((0, 0), (0, 0), (0, wide_part - part)))
    return got.reshape(rows, groups * runs * wide_part)


def return_columns(dealt, here, groups, part, wide_part):
    rows, width = dealt.shape
    runs = width // (groups * wide_part)
    if groups == 4:
        starts = lambda i: [(i * runs + r) * wide_part for r in range(runs)]
        return join_back(exchange(split_columns(dealt, here, starts, part)), here, part)
    pieces = dealt.reshape(rows, groups * runs, wide_part)[:, :, :part]
    got = trade(pieces.reshape(rows, groups, runs * part).transpose(1, 0, 2))
    return got.reshape(groups, rows, runs, part).transpose(1, 2, 0, 3).reshape(rows, -1)


def deal_rows(shard, here, groups, wide_part):
    rows, width = shard.shape
    part = rows // groups
    if groups == 4:
        return join_side(exchange(split_rows(shard, here)), here, wide_part)
    got = trade(shard.reshape(groups, part, width))
    got = got.transpose(1, 0, 2).reshape(part, groups * width)
    return jnp.pad(got, ((0, wide_part - part), (0, 0)))


def return_rows(dealt, here, groups, part):
    width = dealt.shape[1]
    if groups == 4:
        return join_rows(exchange(split_side(dealt, here, part)), here)
    got = trade(dealt[:part].reshape(part, groups, width // groups).transpose(1, 0, 2))
    return got.reshape(groups * part, width // groups)


def beside(pieces, here):
    if len(pieces) != 4:
        return jnp.concatenate(pieces, axis=1)
    return join_side(pieces, here, pieces[0].shape[0])


def apart(values, here, groups):
    if groups != 4:
        return jnp.split(values, groups, axis=1)
    return split_side(values, here, values.shape[0])


def whole(shard):
    return lax.all_gather(shard, "shard", axis=0, tiled=True)


def owned_sum(partial):
    return lax.psum_scatter(partial, "shard", scatter_dimension=0, tiled=True)


def shards(
    groups,
    ranks,
    tokens,
    cotangent,
    lengths,
    step_count,
    norm_gains,
    qkv_weight,
    attn_weight,
    mixer_in,
    mixer_table,
    mixer_out,
    ffn_in,
    ffn_out,
    first_gains,
    first_qkv,
    first_attn,
    first_mixin,
    first_table,
    first_mixout,
    first_ffnin,
    first_ffnout,
    second_gains,
    second_qkv,
    second_attn,
    second_mixin,
    second_table,
    second_mixout,
    second_ffnin,
    second_ffnout,
):
    low = jnp.bfloat16
    buffer_rows = tokens.shape[0]
    model_width = tokens.shape[1]
    at = lax.axis_index("dp")
    here = at.reshape(1)
    part_inner = INNER // groups // ranks
    part_hidden = FF // groups // ranks
    wide_inner = padded_part(part_inner, ranks)
    wide_hidden = padded_part(part_hidden, ranks)
    inner = wide_inner * ranks
    hidden_units = wide_hidden * ranks
    part_model = model_width // ranks
    table_width = mixer_table.shape[1]
    gain_count = norm_gains.shape[1]

    qkv_width = qkv_weight.shape[1]
    attn_width = attn_weight.shape[1]
    table_part = lax.dynamic_slice_in_dim(mixer_table, at * part_inner, part_inner, axis=0)
    table_part = jnp.pad(
        table_part, ((0, part_model - part_inner), (0, 2 * LANES - table_width))
    )
    gain_cols = whole_small(norm_gains.astype(jnp.float32).T, ranks)
    mixer_pack = jnp.concatenate(
        [deal_columns(mixer_in, here, groups, part_inner, wide_inner), table_part], axis=1
    )
    mixer_early = whole(mixer_pack)
    lengths_all = jnp.concatenate(spread_direct(lengths, groups), axis=0)
    owner, offset, live, _ = layout(lengths[0], buffer_rows)
    live_rows = live.astype(jnp.float32)
    places = jnp.arange(buffer_rows, dtype=jnp.int32)
    allowed = (owner[:, None] == owner[None, :]) & (places[None, :] <= places[:, None]) & live[
        None, :
    ] | (places[:, None] == places[None, :])
    _, offset_all, _, begins_all = jax.vmap(lambda row: layout(row, buffer_rows))(lengths_all)
    offset_all = offset_all.reshape(-1)
    block_starts = begins_all[:, ::BLOCK] | (jnp.arange(buffer_rows // BLOCK) == 0)[None, :]
    block_keep = 1.0 - block_starts.reshape(-1).astype(jnp.float32)

    inputs = tokens.astype(jnp.float32)
    scale_in = rms_scale(inputs)
    normed = (inputs * scale_in * gain_cols[0]).astype(low)
    normed_all, near_rows = spread(after(normed, mixer_pack), groups)
    attn_rows = beside(spread_direct(attn_weight, groups), here)
    dealt_mix = deal_rows(after(mixer_out, near_rows), here, groups, wide_inner)
    dealt_up = deal_columns(after(ffn_in, near_rows), here, groups, part_hidden, wide_hidden)
    mixer_full = after(mixer_early, normed_all, dealt_mix, dealt_up)
    weight_in = mixer_full[:, : 2 * inner]
    table_low = mixer_full[:, 2 * inner :].reshape(ranks, part_model, 2 * LANES)[:, :part_inner]
    table_low = jnp.pad(
        table_low[:, :, :table_width], ((0, 0), (0, wide_inner - part_inner), (0, 0))
    ).reshape(inner, table_width)

    heads_full = whole(jnp.concatenate([after(qkv_weight, mixer_full), attn_rows], axis=1))
    weight_qkv, weight_attn = heads_full[:, :qkv_width], heads_full[:, qkv_width:]
    grad_out = cotangent.astype(jnp.float32) * live_rows[:, None]

    mixed = product(normed_all, weight_in)
    weight_mix, weight_up = whole(after(dealt_mix, mixed)), whole(after(dealt_up, mixed))
    xin = mixed[:, :inner]
    gate_z = mixed[:, inner:]
    table = table_low.astype(jnp.float32)
    tap_masks = [(offset_all >= lag).astype(jnp.float32)[:, None] for lag in range(CONV)]
    taps = [shift_rows(xin, lag) * tap_masks[lag] for lag in range(CONV)]
    conv_pre = table[:, CONV]
    for lag in range(CONV):
        conv_pre = conv_pre + table[:, lag] * taps[lag]
    conv_low = silu_act(conv_pre).astype(low)
    conv_out = conv_low.astype(jnp.float32)
    proj_start = CONV + 3 + STATE
    input_proj = table_low[:, proj_start : proj_start + RANK + 2 * STATE]
    step_proj = table_low[:, proj_start + RANK + 2 * STATE :]
    double_part = product_tt(input_proj, conv_low)
    double = everywhere(double_part, groups)
    dealt_down = deal_rows(after(ffn_out, double), here, groups, wide_hidden)
    weight_down = whole(dealt_down)

    heads_part = product(after(normed_all, double_part), weight_qkv).astype(low)
    heads_part = after(heads_part, double)
    heads_low = beside(exchange(row_pieces(heads_part, groups)), here)
    kv_width = KV * HEAD
    query = heads_low[:, :model_width].reshape(buffer_rows, KV, GROUP, HEAD)
    key_rows = heads_low[:, model_width : model_width + kv_width].reshape(buffer_rows, KV, HEAD)
    value_rows = heads_low[:, model_width + kv_width :].reshape(buffer_rows, KV, HEAD)
    factor = HEAD ** (-0.5)

    def masked_scores():
        raw_scores = (
            jnp.einsum("qkgd,skd->kgqs", query, key_rows, preferred_element_type=jnp.float32)
            * factor
        )
        return jnp.where(allowed, raw_scores, masked_score)

    scores = masked_scores()
    top_score = jnp.max(scores, axis=-1, keepdims=True)
    log_total = top_score + jnp.log(jnp.sum(jnp.exp(scores - top_score), axis=-1, keepdims=True))
    probs_low = jnp.exp(scores - log_total).astype(low)
    context = (
        jnp.einsum("kgqs,skd->qkgd", probs_low, value_rows, preferred_element_type=jnp.float32)
        .reshape(buffer_rows, model_width)
        .astype(low)
    )
    attn_raw = product(context, weight_attn)
    scale_attn = rms_scale(attn_raw)

    rank_part = double[:RANK].astype(low)
    inject = double[RANK : RANK + STATE]
    readout = double[RANK + STATE :]
    dt_pre = product_tt(rank_part, step_proj) + table[:, CONV + 1]
    step_size = jnp.log1p(jnp.exp(dt_pre))
    rates = -jnp.exp(table[:, CONV + 3 : CONV + 3 + STATE]).T
    states_out, block_begins, inject_wide, readout_wide = scan_forward(
        block_keep, step_size, conv_out, inject, readout, rates
    )
    skip_weight = table[:, CONV + 2]
    scanned = states_out + skip_weight * conv_out
    silu_z = silu_act(gate_z)
    gated_low = (scanned * silu_z).astype(low)
    gated_low = after(gated_low, heads_low, dealt_down)
    mamba_raw = collect(row_pieces(product(gated_low, weight_mix).astype(low), groups))
    mamba_raw = after(mamba_raw, attn_raw)
    scale_mamba = rms_scale(mamba_raw)
    hidden = inputs + 0.5 * (
        attn_raw * scale_attn * gain_cols[1] + mamba_raw * scale_mamba * gain_cols[2]
    )
    scale_hidden = rms_scale(hidden)
    normed_two = (hidden * scale_hidden * gain_cols[3]).astype(low)

    normed_two_all, _ = spread(normed_two, groups)
    grad_ffn_pieces = spread_direct(after(grad_out.astype(low), normed_two_all), groups)
    both = product(normed_two_all, weight_up)
    both, grad_ffn_pieces = lax.optimization_barrier((both, grad_ffn_pieces))
    grad_ffn_all = jnp.concatenate(grad_ffn_pieces, axis=0)
    gate_ffn = both[:, :hidden_units]
    up_ffn = both[:, hidden_units:]
    act_low = (silu_act(gate_ffn) * up_ffn).astype(low)
    grad_act = product_nt(grad_ffn_all, weight_down)
    gate_sig = sigmoid(gate_ffn)
    grad_gate = grad_act * up_ffn * gate_sig * (1.0 + gate_ffn * (1.0 - gate_sig))
    grad_up = grad_act * silu_act(gate_ffn)
    grad_both = jnp.concatenate([grad_gate, grad_up], axis=1).astype(low)
    grad_second = product_nt(grad_both, weight_up).astype(low)
    grad_up_w = product_tn(after(normed_two_all, grad_second), grad_both).astype(low)
    grad_down_w = product_tn(act_low, after(grad_ffn_all, grad_up_w)).astype(low)
    grad_second = collect(row_pieces(grad_second, groups))
    grad_second = after(grad_second, grad_up_w, grad_down_w)
    back_hidden, gain_three = rms_back(hidden, scale_hidden, gain_cols[3], grad_second)
    grad_hidden = grad_out + back_hidden
    half_grad = 0.5 * grad_hidden
    grad_mamba_full, gain_two = rms_back(mamba_raw, scale_mamba, gain_cols[2], half_grad)
    grad_mamba_all, _ = spread(grad_mamba_full.astype(low), groups)
    up_own, down_own = owned_sum(grad_up_w), owned_sum(grad_down_w)

    grad_attn_full, gain_one = rms_back(attn_raw, scale_attn, gain_cols[1], half_grad)
    grad_attn_low = grad_attn_full.astype(low)
    grad_context = (
        product_nt(grad_attn_low, weight_attn).astype(low).reshape(buffer_rows, KV, GROUP, HEAD)
    )
    probs_again = jnp.exp(masked_scores() - log_total)
    grad_probs = jnp.einsum(
        "qkgd,skd->kgqs", grad_context, value_rows, preferred_element_type=jnp.float32
    )
    grad_values = jnp.einsum(
        "kgqs,qkgd->skd",
        probs_again.astype(low),
        grad_context,
        preferred_element_type=jnp.float32,
    )
    grad_scores = (
        probs_again * (grad_probs - jnp.sum(probs_again * grad_probs, axis=-1, keepdims=True))
    ).astype(low)
    grad_query = (
        jnp.einsum("kgqs,skd->qkgd", grad_scores, key_rows, preferred_element_type=jnp.float32)
        * factor
    )
    grad_keys = (
        jnp.einsum("kgqs,qkgd->skd", grad_scores, query, preferred_element_type=jnp.float32)
        * factor
    )
    grad_heads = jnp.concatenate(
        [
            grad_query.reshape(buffer_rows, model_width),
            grad_keys.reshape(buffer_rows, kv_width),
            grad_values.reshape(buffer_rows, kv_width),
        ],
        axis=1,
    ).astype(low)
    grad_heads_part = jnp.concatenate(exchange(apart(grad_heads, here, groups)), axis=0)

    grad_mamba_all = after(grad_mamba_all, grad_heads)
    grad_gated = product_nt(grad_mamba_all, weight_mix)
    grad_scanned = grad_gated * silu_z
    grad_gate_low = (grad_gated * scanned * silu_slope(gate_z)).astype(low)
    grad_mix_w = product_tn(gated_low, grad_mamba_all).astype(low)
    grad_gate_w = product_tn(normed_all, grad_gate_low).astype(low)
    mix_own, gate_own = owned_sum(grad_mix_w), owned_sum(grad_gate_w)
    heads_pack = jnp.concatenate(
        [
            product_tn(normed_all, grad_heads_part).astype(low),
            product_tn(context, grad_attn_low).astype(low),
        ],
        axis=1,
    )
    heads_own = owned_sum(heads_pack)
    raw_pieces = row_pieces(product(after(act_low, grad_gate_w), weight_down).astype(low), groups)
    grad_scanned, raw_pieces = after(
        (grad_scanned, raw_pieces), grad_mix_w, grad_gate_w, heads_pack
    )
    raw_hops = first_hop(raw_pieces)
    grad_skip = jnp.sum(grad_scanned * conv_out, axis=0)
    grad_step, grad_conv_scan, grad_inject, grad_readout, grad_rates = scan_backward(
        block_keep,
        step_size,
        conv_out,
        inject_wide,
        readout_wide,
        rates,
        grad_scanned,
        block_begins,
    )
    grad_step = after(grad_step, up_own, raw_hops)
    grad_pre = grad_step * sigmoid(dt_pre)
    grad_step_bias = jnp.sum(grad_pre, axis=0)
    grad_pre_low = grad_pre.astype(low)
    grad_rank = product_tt(step_proj, grad_pre_low)
    grad_double = everywhere(
        jnp.concatenate([grad_rank, grad_inject, grad_readout], axis=0), groups
    ).astype(low)

    raw_hops = after(raw_hops, grad_double)
    ffn_raw = second_hop(raw_pieces, raw_hops)
    output = (live_rows[:, None] * (hidden + ffn_raw)).astype(low)
    grad_conv_out = (
        product_tt(grad_double, input_proj) + grad_conv_scan + skip_weight * grad_scanned
    )
    grad_conv_out = after(grad_conv_out, down_own, mix_own)
    grad_conv = grad_conv_out * silu_slope(conv_pre)
    grad_xin = unshift_rows(grad_conv * tap_masks[0] * table[:, 0], 0)
    for lag in range(1, CONV):
        grad_xin = grad_xin + unshift_rows(grad_conv * tap_masks[lag] * table[:, lag], lag)
    grad_xin_low = grad_xin.astype(low)
    grad_table = jnp.concatenate(
        [
            jnp.stack(
                [jnp.sum(grad_conv * taps[lag], axis=0) for lag in range(CONV)]
                + [jnp.sum(grad_conv, axis=0), grad_step_bias, grad_skip]
            ),
            grad_rates * rates,
            product(grad_double, conv_low),
            product(rank_part, grad_pre_low),
            jnp.zeros((2 * LANES - table_width, inner), jnp.float32),
        ],
        axis=0,
    ).astype(low)
    grad_table = jnp.pad(
        grad_table.T.reshape(ranks, wide_inner, 2 * LANES),
        ((0, 0), (0, part_model - wide_inner), (0, 0)),
    ).reshape(model_width, 2 * LANES)
    xin_pack = jnp.concatenate(
        [product_tn(normed_all, grad_xin_low).astype(low), grad_table], axis=1
    )
    xin_pack = after(xin_pack, gate_own)
    last_own = owned_sum(xin_pack)
    normed_part = (
        product_nt(grad_heads_part, weight_qkv)
        + product_nt(grad_gate_low, weight_in[:, inner:])
        + product_nt(after(grad_xin_low, xin_pack), weight_in[:, :inner])
    ).astype(low)
    grad_normed = collect(row_pieces(normed_part, groups))
    back_inputs, gain_zero = rms_back(inputs, scale_in, gain_cols[0], grad_normed)
    grad_tokens = grad_hidden + back_inputs
    grad_gains = everyone(jnp.stack([gain_zero, gain_one, gain_two, gain_three], axis=0), groups, ranks)
    grad_gains_done = lax.dynamic_slice_in_dim(
        grad_gains, lax.axis_index("shard") * part_model, part_model, axis=1
    ).T

    last_own = lax.optimization_barrier(last_own)
    heads_own = lax.optimization_barrier(heads_own)
    grad_in_done = return_columns(
        jnp.concatenate([last_own[:, :inner], gate_own], axis=1),
        here,
        groups,
        part_inner,
        wide_inner,
    )
    table_pieces = spread_direct(last_own[:part_inner, inner : inner + 2 * LANES], groups)
    if groups == 4:
        grad_table_done = join_rows(table_pieces, here)[:, :table_width]
    else:
        grad_table_done = jnp.concatenate(table_pieces, axis=0)[:, :table_width]
    grad_qkv_done = heads_own[:, :qkv_width]
    grad_attn_done = sum(
        piece.astype(jnp.float32)
        for piece in exchange(apart(heads_own[:, qkv_width:], here, groups))
    )
    grad_mix_done = return_rows(after(mix_own, normed_part), here, groups, part_inner)
    ffn_done = (
        return_columns(after(up_own, normed_part), here, groups, part_hidden, wide_hidden),
        return_rows(after(down_own, normed_part), here, groups, part_hidden),
    )

    owned = (norm_gains, qkv_weight, attn_weight, mixer_in, mixer_table, mixer_out, ffn_in, ffn_out)
    grads_owned = (
        grad_gains_done,
        grad_qkv_done,
        grad_attn_done,
        grad_in_done,
        grad_table_done,
        grad_mix_done,
        ffn_done[0],
        ffn_done[1],
    )
    firsts = (
        first_gains,
        first_qkv,
        first_attn,
        first_mixin,
        first_table,
        first_mixout,
        first_ffnin,
        first_ffnout,
    )
    seconds = (
        second_gains,
        second_qkv,
        second_attn,
        second_mixin,
        second_table,
        second_mixout,
        second_ffnin,
        second_ffnout,
    )
    step_float = step_count[0].astype(jnp.float32)
    updates = [
        adam_rows(owned[slot], grads_owned[slot], firsts[slot], seconds[slot], step_float)
        for slot in range(8)
    ]
    return (output, grad_tokens) + tuple(entry[kind] for kind in range(4) for entry in updates)


def solution(mesh):
    in_specs = (
        P(("dp", "shard"), None),
        P(("dp", "shard"), None),
        P(("dp", "shard"), None),
        P(),
        P("shard", None),
        P("shard", "dp"),
        P("shard", "dp"),
        P("shard", "dp"),
        P("shard", None),
        P("shard", "dp"),
        P("shard", "dp"),
        P("shard", "dp"),
        P("shard", None),
        P("shard", "dp"),
        P("shard", "dp"),
        P("shard", "dp"),
        P("shard", None),
        P("shard", "dp"),
        P("shard", "dp"),
        P("shard", "dp"),
        P("shard", None),
        P("shard", "dp"),
        P("shard", "dp"),
        P("shard", "dp"),
        P("shard", None),
        P("shard", "dp"),
        P("shard", "dp"),
        P("shard", "dp"),
    )
    out_specs = (
        P(("dp", "shard"), None),
        P(("dp", "shard"), None),
        P("shard", None),
        P("shard", "dp"),
        P("shard", "dp"),
        P("shard", "dp"),
        P("shard", None),
        P("shard", "dp"),
        P("shard", "dp"),
        P("shard", "dp"),
        P("shard", None),
        P("shard", "dp"),
        P("shard", "dp"),
        P("shard", "dp"),
        P("shard", None),
        P("shard", "dp"),
        P("shard", "dp"),
        P("shard", "dp"),
        P("shard", None),
        P("shard", "dp"),
        P("shard", "dp"),
        P("shard", "dp"),
        P("shard", None),
        P("shard", "dp"),
        P("shard", "dp"),
        P("shard", "dp"),
        P("shard", None),
        P("shard", "dp"),
        P("shard", "dp"),
        P("shard", "dp"),
        P("shard", None),
        P("shard", "dp"),
        P("shard", "dp"),
        P("shard", "dp"),
    )
    return jax.shard_map(functools.partial(shards, mesh.shape["dp"], mesh.shape["shard"]), mesh=mesh, in_specs=in_specs, out_specs=out_specs, check_vma=False)
```

```python
import functools

import jax
import jax.numpy as jnp
from jax import lax
from jax.experimental import pallas as pl
from jax.experimental.pallas import tpu as pltpu
from jax.sharding import PartitionSpec as P

KV = 5
HEAD = 64
GROUP = 5
INNER = 3200
STATE = 16
CONV = 4
RANK = 100
FF = 5504
BLOCK = 128
LANES = 128


epsilon = 1e-06
beta_first = 0.9
beta_second = 0.95
adam_floor = 1e-08
learn_rate = 0.01
weight_decay = 0.1
masked_score = -1e30


def product(left, right):
    return jnp.dot(left, right, preferred_element_type=jnp.float32)


def product_tn(left, right):
    return lax.dot_general(
        left, right, (((0,), (0,)), ((), ())), preferred_element_type=jnp.float32
    )


def product_nt(left, right):
    return lax.dot_general(
        left, right, (((1,), (1,)), ((), ())), preferred_element_type=jnp.float32
    )


def sigmoid(values):
    return 1.0 / (1.0 + jnp.exp(-values))


def silu_act(values):
    return values / (1.0 + jnp.exp(-values))


def silu_slope(values):
    gate_sig = sigmoid(values)
    return gate_sig * (1.0 + values * (1.0 - gate_sig))


def rms_scale(values):
    return lax.rsqrt(jnp.mean(values * values, axis=-1, keepdims=True) + epsilon)


def rms_back(values, scale, gain, incoming):
    weighted = incoming * gain
    inner_mean = jnp.mean(weighted * values, axis=-1, keepdims=True)
    return (
        scale * weighted - values * (scale * scale * scale) * inner_mean,
        jnp.sum(incoming * values * scale, axis=0),
    )


def shift_rows(values, lag):
    if lag == 0:
        return values
    return jnp.concatenate(
        [jnp.zeros((lag, values.shape[1]), values.dtype), values[: values.shape[0] - lag]], axis=0
    )


def unshift_rows(values, lag):
    if lag == 0:
        return values
    return jnp.concatenate([values[lag:], jnp.zeros((lag, values.shape[1]), values.dtype)], axis=0)


def row_sums(parts):
    rows = lax.broadcasted_iota(jnp.int32, (8, LANES), 0)
    quads = []
    low = rows < 4
    for i in range(4):
        a, b = parts[i], parts[i + 4]
        quads.append(jnp.where(low, a, b) + pltpu.roll(jnp.where(low, b, a), 4, 0))
    pairs = []
    low = (rows & 3) < 2
    for i in range(2):
        a, b = quads[i], quads[i + 2]
        pairs.append(jnp.where(low, a + pltpu.roll(a, 6, 0), b + pltpu.roll(b, 2, 0)))
    a, b = pairs
    return jnp.where((rows & 1) < 1, a + pltpu.roll(a, 7, 0), b + pltpu.roll(b, 1, 0))


def fold_rows_in(values):
    return values[:8] + values[8:]


def lane_tiles(width):
    return [slice(k * LANES, (k + 1) * LANES) for k in range(width // LANES)]


def scan_kernel(
    keep_ref,
    step_ref,
    conv_ref,
    inject_ref,
    read_ref,
    rates_ref,
    gate_ref,
    channel_ref,
    out_ref,
    gated_ref,
    start_ref,
    inject_wide_ref,
    read_wide_ref,
    state_ref,
):
    at = pl.program_id(0)
    tiles = lane_tiles(step_ref.shape[1])

    @pl.when(at == 0)
    def _():
        state_ref[...] = jnp.zeros_like(state_ref)

    state_ref[...] = state_ref[...] * keep_ref[at]
    start_ref[0] = state_ref[...]
    rates = [rates_ref[:, tile] for tile in tiles]

    def group(turn, state):
        base = pl.multiple_of(turn * 8, 8)
        state = list(state)
        steps = [step_ref[pl.ds(base, 8), tile] for tile in tiles]
        pushes = [
            steps[k] * conv_ref[pl.ds(base, 8), tile] for k, tile in enumerate(tiles)
        ]
        parts = [[] for _ in tiles]
        turned = [pltpu.roll(ref[...], BLOCK - base, 1) for ref in (inject_ref, read_ref)]
        for i in range(8):
            inject, read = [
                jnp.broadcast_to(values[:, i : i + 1], (STATE, LANES)) for values in turned
            ]
            inject_wide_ref[base + i], read_wide_ref[base + i] = inject, read
            for k in range(len(tiles)):
                decay = jnp.exp(steps[k][i : i + 1] * rates[k])
                state[k] = decay * state[k] + pushes[k][i : i + 1] * inject
                parts[k].append(fold_rows_in(state[k] * read))
        for k, tile in enumerate(tiles):
            out_ref[pl.ds(base, 8), tile] = row_sums(parts[k])
        return tuple(state)

    state = lax.fori_loop(0, BLOCK // 8, group, tuple(state_ref[:, tile] for tile in tiles))
    for k, tile in enumerate(tiles):
        state_ref[:, tile] = state[k]
        scanned = out_ref[:, tile] + channel_ref[CONV + 2 : CONV + 3, tile] * conv_ref[:, tile]
        out_ref[:, tile] = scanned
        gated_ref[:, tile] = (scanned * silu_act(gate_ref[:, tile])).astype(jnp.bfloat16)


def scan_forward(keep, step, conv, inject, read, rates, mixed, channels):
    rows, width = step.shape
    blocks = rows // BLOCK
    row_spec = pl.BlockSpec((BLOCK, width), lambda i, *_: (i, 0))
    state_spec = pl.BlockSpec((STATE, BLOCK), lambda i, *_: (0, i))
    wide_spec = pl.BlockSpec((BLOCK, STATE, LANES), lambda i, *_: (i, 0, 0))
    return pl.pallas_call(
        scan_kernel,
        grid_spec=pltpu.PrefetchScalarGridSpec(
            num_scalar_prefetch=1,
            grid=(blocks,),
            in_specs=[
                row_spec,
                row_spec,
                state_spec,
                state_spec,
                pl.BlockSpec((STATE, width), lambda i, *_: (0, 0)),
                pl.BlockSpec((BLOCK, width), lambda i, *_: (i, 1)),
                pl.BlockSpec((8, width), lambda i, *_: (0, 0)),
            ],
            out_specs=[
                row_spec,
                row_spec,
                pl.BlockSpec((1, STATE, width), lambda i, *_: (i, 0, 0)),
                wide_spec,
                wide_spec,
            ],
            scratch_shapes=[pltpu.VMEM((STATE, width), jnp.float32)],
        ),
        out_shape=[
            jax.ShapeDtypeStruct((rows, width), jnp.float32),
            jax.ShapeDtypeStruct((rows, width), jnp.bfloat16),
            jax.ShapeDtypeStruct((blocks, STATE, width), jnp.float32),
        ]
        + [jax.ShapeDtypeStruct((rows, STATE, LANES), jnp.float32)] * 2,
        cost_estimate=pl.CostEstimate(
            flops=30 * rows * STATE * width,
            bytes_accessed=140 * rows * width,
            transcendentals=rows * STATE * width,
        ),
        compiler_params=pltpu.CompilerParams(vmem_limit_bytes=24 * 2**20),
        name="state_scan",
    )(keep, step, conv, inject, read, rates, mixed, channels)


def back_kernel(
    keep_ref,
    step_ref,
    conv_ref,
    inject_ref,
    read_ref,
    rates_ref,
    gated_ref,
    gate_ref,
    scanned_ref,
    pre_ref,
    start_ref,
    grad_ref,
    ggate_ref,
    gpre_ref,
    gconv_ref,
    ginject_ref,
    gread_ref,
    grate_ref,
    gsums_ref,
    later_ref,
    history_ref,
    decay_ref,
    sums_ref,
    gstep_ref,
):
    tiles = lane_tiles(step_ref.shape[1])
    at = pl.num_programs(0) - 1 - pl.program_id(0)

    @pl.when(pl.program_id(0) == 0)
    def _():
        later_ref[...] = jnp.zeros_like(later_ref)
        grate_ref[...] = jnp.zeros_like(grate_ref)
        gsums_ref[...] = jnp.zeros_like(gsums_ref)

    for tile in tiles:
        gate, incoming = gate_ref[:, tile], gated_ref[:, tile]
        opened = sigmoid(gate)
        grad = incoming * (gate * opened)
        grad_ref[:, tile] = grad
        slope = opened * (1.0 + gate * (1.0 - opened))
        ggate_ref[:, tile] = (incoming * scanned_ref[:, tile] * slope).astype(jnp.bfloat16)
        gsums_ref[0:1, tile] += jnp.sum(grad * conv_ref[:, tile], axis=0, keepdims=True)

    def forward(turn, state):
        base = pl.multiple_of(turn * 8, 8)
        state = list(state)
        steps = [step_ref[pl.ds(base, 8), tile] for tile in tiles]
        pushes = [
            steps[k] * conv_ref[pl.ds(base, 8), tile] for k, tile in enumerate(tiles)
        ]
        for i in range(8):
            inject = inject_ref[base + i]
            for k, tile in enumerate(tiles):
                decay = jnp.exp(steps[k][i : i + 1] * rates_ref[:, tile])
                decay_ref[base + i, :, tile] = decay
                history_ref[base + i, :, tile] = state[k]
                state[k] = decay * state[k] + pushes[k][i : i + 1] * inject
        return tuple(state)

    state = lax.fori_loop(
        0, BLOCK // 8, forward, tuple(start_ref[0, :, tile] for tile in tiles)
    )
    for k, tile in enumerate(tiles):
        history_ref[BLOCK, :, tile] = state[k]

    def backward(turn, later):
        base = pl.multiple_of((BLOCK // 8 - 1 - turn) * 8, 8)
        later = list(later)
        steps = [step_ref[pl.ds(base, 8), tile] for tile in tiles]
        convs = [conv_ref[pl.ds(base, 8), tile] for tile in tiles]
        grads = [grad_ref[pl.ds(base, 8), tile] for tile in tiles]
        pushes = [steps[k] * convs[k] for k in range(len(tiles))]
        pulls = [[None] * 8 for _ in tiles]
        drives = [[None] * 8 for _ in tiles]
        rate_sums = [None for _ in tiles]
        for i in range(7, -1, -1):
            sums = [None, None]
            inject, read = inject_ref[base + i], read_ref[base + i]
            for k, tile in enumerate(tiles):
                grad = grads[k][i : i + 1]
                total = read * grad + later[k]
                later[k] = decay_ref[base + i, :, tile] * total
                pull = later[k] * history_ref[base + i, :, tile]
                pulls[k][i] = fold_rows_in(pull * rates_ref[:, tile])
                drives[k][i] = fold_rows_in(total * inject)
                terms = [total * pushes[k][i : i + 1], history_ref[base + i + 1, :, tile] * grad]
                sums = [term if old is None else old + term for old, term in zip(sums, terms)]
                term = pull * steps[k][i : i + 1]
                rate_sums[k] = term if rate_sums[k] is None else rate_sums[k] + term
            sums_ref[0, base + i], sums_ref[1, base + i] = sums
        for k, tile in enumerate(tiles):
            grate_ref[:, tile] += rate_sums[k]
            drive = row_sums(drives[k])
            gstep_ref[pl.ds(base, 8), tile] = row_sums(pulls[k]) + drive * convs[k]
            gconv_ref[pl.ds(base, 8), tile] = drive * steps[k]
        return tuple(later)

    later = lax.fori_loop(
        0, BLOCK // 8, backward, tuple(later_ref[:, tile] for tile in tiles)
    )
    for tile in tiles:
        grad = gstep_ref[:, tile] * sigmoid(pre_ref[:, tile])
        gpre_ref[:, tile] = grad.astype(jnp.bfloat16)
        gsums_ref[1:2, tile] += jnp.sum(grad, axis=0, keepdims=True)
    ones = jnp.ones((LANES, LANES), jnp.bfloat16)
    lane = lax.broadcasted_iota(jnp.int32, (STATE, BLOCK), 1)
    ginject_ref[...] = jnp.zeros_like(ginject_ref)
    gread_ref[...] = jnp.zeros_like(gread_ref)

    def lane_sums(turn, none):
        base = pl.multiple_of(turn * 32, 32)
        for which, ref in enumerate((ginject_ref, gread_ref)):
            values = sums_ref[which, pl.ds(base, 32)].reshape(32 * STATE, LANES)
            high = values.astype(jnp.bfloat16)
            rest = (values - high.astype(jnp.float32)).astype(jnp.bfloat16)
            totals = jnp.dot(high, ones, preferred_element_type=jnp.float32) + jnp.dot(
                rest, ones, preferred_element_type=jnp.float32
            )
            kept = ref[...]
            for i in range(32):
                kept = jnp.where(lane == base + i, totals[i * STATE : (i + 1) * STATE], kept)
            ref[...] = kept
        return none

    lax.fori_loop(0, BLOCK // 32, lane_sums, 0)
    for k, tile in enumerate(tiles):
        later_ref[:, tile] = later[k] * keep_ref[at]


def scan_backward(keep, step, conv, inject, read, rates, grad_gated, mixed, scanned, pre, starts):
    rows, width = step.shape
    blocks = rows // BLOCK
    row_spec = pl.BlockSpec((BLOCK, width), lambda i, *_: (blocks - 1 - i, 0))
    wide_spec = pl.BlockSpec((BLOCK, STATE, LANES), lambda i, *_: (blocks - 1 - i, 0, 0))
    all_spec = pl.BlockSpec((STATE, width), lambda i, *_: (0, 0))
    flat_spec = pl.BlockSpec((STATE, BLOCK), lambda i, *_: (0, blocks - 1 - i))
    return pl.pallas_call(
        back_kernel,
        grid_spec=pltpu.PrefetchScalarGridSpec(
            num_scalar_prefetch=1,
            grid=(blocks,),
            in_specs=[
                row_spec,
                row_spec,
                wide_spec,
                wide_spec,
                all_spec,
                row_spec,
                pl.BlockSpec((BLOCK, width), lambda i, *_: (blocks - 1 - i, 1)),
                row_spec,
                row_spec,
                pl.BlockSpec((1, STATE, width), lambda i, *_: (blocks - 1 - i, 0, 0)),
            ],
            out_specs=[row_spec] * 4
            + [flat_spec, flat_spec, all_spec, pl.BlockSpec((8, width), lambda i, *_: (0, 0))],
            scratch_shapes=[
                pltpu.VMEM((STATE, width), jnp.float32),
                pltpu.VMEM((BLOCK + 1, STATE, width), jnp.float32),
                pltpu.VMEM((BLOCK, STATE, width), jnp.float32),
                pltpu.VMEM((2, BLOCK, STATE, LANES), jnp.float32),
                pltpu.VMEM((BLOCK, width), jnp.float32),
            ],
        ),
        out_shape=[
            jax.ShapeDtypeStruct((rows, width), kind)
            for kind in (jnp.float32, jnp.bfloat16, jnp.bfloat16, jnp.float32)
        ]
        + [jax.ShapeDtypeStruct((STATE, rows), jnp.float32)] * 2
        + [jax.ShapeDtypeStruct((n, width), jnp.float32) for n in (STATE, 8)],
        cost_estimate=pl.CostEstimate(
            flops=60 * rows * STATE * width,
            bytes_accessed=260 * rows * width,
            transcendentals=rows * STATE * width,
        ),
        compiler_params=pltpu.CompilerParams(vmem_limit_bytes=48 * 2**20),
        name="state_back",
    )(keep, step, conv, inject, read, rates, grad_gated, mixed, scanned, pre, starts)


def conv_kernel(mixed_ref, place_ref, channel_ref, pre_ref, out_ref, low_ref):
    inputs, place = mixed_ref[...], place_ref[...]
    total = channel_ref[CONV : CONV + 1] + channel_ref[0:1] * inputs
    for lag in range(1, CONV):
        tap = jnp.where(place >= lag, pltpu.roll(inputs, lag, 0), 0.0)
        total = total + channel_ref[lag : lag + 1] * tap
    pre_ref[...] = total
    low = silu_act(total).astype(jnp.bfloat16)
    low_ref[...] = low
    out_ref[...] = low.astype(jnp.float32)


def conv_forward(mixed, place, channels):
    rows, width = mixed.shape[0], channels.shape[1]
    spec = pl.BlockSpec((rows, LANES), lambda i: (0, i))
    return pl.pallas_call(
        conv_kernel,
        grid=(width // LANES,),
        in_specs=[
            spec,
            pl.BlockSpec((rows, LANES), lambda i: (0, 0)),
            pl.BlockSpec((8, LANES), lambda i: (0, i)),
        ],
        out_specs=[spec] * 3,
        out_shape=[
            jax.ShapeDtypeStruct((rows, width), kind)
            for kind in (jnp.float32, jnp.float32, jnp.bfloat16)
        ],
        compiler_params=pltpu.CompilerParams(vmem_limit_bytes=24 * 2**20),
        name="conv_forward",
    )(mixed, place, channels)


def conv_back_kernel(
    part_ref, scan_ref, grad_ref, pre_ref, mixed_ref, place_ref, channel_ref, low_ref, sums_ref
):
    pre, inputs, place = pre_ref[...], mixed_ref[...], place_ref[...]
    rows = pre.shape[0]
    grad = part_ref[...] + scan_ref[...] + channel_ref[CONV + 2 : CONV + 3] * grad_ref[...]
    grad = grad * silu_slope(pre)
    sums_ref[CONV : CONV + 1] = jnp.sum(grad, axis=0, keepdims=True)
    sums_ref[0:1] = jnp.sum(grad * inputs, axis=0, keepdims=True)
    total = channel_ref[0:1] * grad
    for lag in range(1, CONV):
        kept = jnp.where(place >= lag, grad, 0.0)
        sums_ref[lag : lag + 1] = jnp.sum(kept * pltpu.roll(inputs, lag, 0), axis=0, keepdims=True)
        total = total + pltpu.roll(channel_ref[lag : lag + 1] * kept, rows - lag, 0)
    sums_ref[CONV + 1 :] = jnp.zeros((7 - CONV, LANES), jnp.float32)
    low_ref[...] = total.astype(jnp.bfloat16)


def conv_backward(part, scan, grad, pre, mixed, place, channels):
    rows, width = pre.shape
    spec = pl.BlockSpec((rows, LANES), lambda i: (0, i))
    few = pl.BlockSpec((8, LANES), lambda i: (0, i))
    return pl.pallas_call(
        conv_back_kernel,
        grid=(width // LANES,),
        in_specs=[spec] * 5 + [pl.BlockSpec((rows, LANES), lambda i: (0, 0)), few],
        out_specs=[spec, few],
        out_shape=[
            jax.ShapeDtypeStruct((rows, width), jnp.bfloat16),
            jax.ShapeDtypeStruct((8, width), jnp.float32),
        ],
        compiler_params=pltpu.CompilerParams(vmem_limit_bytes=24 * 2**20),
        name="conv_backward",
    )(part, scan, grad, pre, mixed, place, channels)


def adam_kernel(
    fix_ref, weight_ref, grad_ref, first_ref, second_ref, out_ref, mean_ref, square_ref, delta_ref
):
    gradient = grad_ref[...].astype(jnp.float32)
    out_ref[...] = gradient
    mean_new = beta_first * first_ref[...] + (1.0 - beta_first) * gradient
    square_new = beta_second * second_ref[...] + (1.0 - beta_second) * gradient * gradient
    mean_ref[...] = mean_new
    square_ref[...] = square_new
    delta_ref[...] = -learn_rate * (
        mean_new / fix_ref[0] / (jnp.sqrt(square_new / fix_ref[1]) + adam_floor)
        + weight_decay * weight_ref[...].astype(jnp.float32)
    )


def adam_rows(weight, gradient, first_old, second_old, step_float):
    rows, width = weight.shape
    across = -(-rows // LANES) * LANES * width < -(-width // LANES) * LANES * rows
    operands = (weight, gradient, first_old, second_old)
    if across:
        operands = tuple(values.T for values in operands)
        rows, width = width, rows
    sizes = [n for n in range(8, rows, 8) if rows % n == 0 and n * width <= 2**17]
    size = max(sizes, default=rows)
    fixes = jnp.stack(
        [1.0 - jnp.power(beta_first, step_float), 1.0 - jnp.power(beta_second, step_float)]
    )
    spec = pl.BlockSpec((size, width), lambda i, *_: (i, 0))
    results = pl.pallas_call(
        adam_kernel,
        grid_spec=pltpu.PrefetchScalarGridSpec(
            num_scalar_prefetch=1, grid=(rows // size,), in_specs=[spec] * 4, out_specs=[spec] * 4
        ),
        out_shape=[jax.ShapeDtypeStruct((rows, width), jnp.float32)] * 4,
        cost_estimate=pl.CostEstimate(
            flops=20 * rows * width, bytes_accessed=28 * rows * width, transcendentals=rows * width
        ),
        compiler_params=pltpu.CompilerParams(vmem_limit_bytes=16 * 2**20),
        name="adam_rows",
    )(fixes, *operands)
    return [values.T for values in results] if across else results


def by_place(body):
    def kernel(here_ref, *refs):
        for here in range(4):
            pl.when(here_ref[0] == here)(functools.partial(body, here, *refs))

    return kernel


def column_runs(values, starts, width, padding=0):
    parts = []
    for start in starts:
        parts.append(values[:, start : start + width])
        if padding:
            parts.append(jnp.zeros((values.shape[0], padding), values.dtype))
    return jnp.concatenate(parts, axis=1)


def place_call(body, here, operands, shapes, name):
    return pl.pallas_call(
        by_place(body),
        grid_spec=pltpu.PrefetchScalarGridSpec(
            num_scalar_prefetch=1,
            in_specs=[pl.BlockSpec(memory_space=pltpu.VMEM)] * len(operands),
            out_specs=[pl.BlockSpec(memory_space=pltpu.VMEM)] * len(shapes),
        ),
        out_shape=shapes,
        compiler_params=pltpu.CompilerParams(vmem_limit_bytes=24 * 2**20),
        name=name,
    )(here, *operands)


def split_columns(shard, here, starts_of, width):
    count = len(starts_of(0)) * width

    def body(here, shard_ref, *piece_refs):
        values = shard_ref[...].astype(jnp.float32)
        for j, ref in enumerate(piece_refs):
            ref[...] = column_runs(values, starts_of(here ^ j), width).astype(ref.dtype)

    shapes = [jax.ShapeDtypeStruct((shard.shape[0], count), shard.dtype)] * 4
    return place_call(body, here, [shard], shapes, "split_columns")


def join_columns(pieces, here, width, wide):
    rows, count = pieces[0].shape
    runs = count // width

    def body(here, *refs):
        values = [ref[...].astype(jnp.float32) for ref in refs[:4]]
        refs[4][...] = jnp.concatenate(
            [
                column_runs(values[here ^ i], [r * width for r in range(runs)], width, wide - width)
                for i in range(4)
            ],
            axis=1,
        ).astype(refs[4].dtype)

    shape = jax.ShapeDtypeStruct((rows, 4 * runs * wide), pieces[0].dtype)
    return place_call(body, here, pieces, [shape], "join_columns")[0]


def split_rows(shard, here):
    part = shard.shape[0] // 4

    def body(here, shard_ref, *piece_refs):
        values = shard_ref[...].astype(jnp.float32)
        for j, ref in enumerate(piece_refs):
            i = here ^ j
            ref[...] = values[i * part : (i + 1) * part].astype(ref.dtype)

    shapes = [jax.ShapeDtypeStruct((part, shard.shape[1]), shard.dtype)] * 4
    return place_call(body, here, [shard], shapes, "split_rows")


def join_side(pieces, here, wide):
    part, width = pieces[0].shape

    def body(here, *refs):
        values = jnp.concatenate(
            [refs[here ^ i][...].astype(jnp.float32) for i in range(4)], axis=1
        )
        refs[4][:part] = values.astype(refs[4].dtype)
        if wide > part:
            refs[4][part:] = jnp.zeros((wide - part, 4 * width), refs[4].dtype)

    shape = jax.ShapeDtypeStruct((wide, 4 * width), pieces[0].dtype)
    return place_call(body, here, pieces, [shape], "join_side")[0]


def split_side(dealt, here, part):
    width = dealt.shape[1] // 4

    def body(here, dealt_ref, *piece_refs):
        values = dealt_ref[:part].astype(jnp.float32)
        for j, ref in enumerate(piece_refs):
            i = here ^ j
            ref[...] = values[:, i * width : (i + 1) * width].astype(ref.dtype)

    shapes = [jax.ShapeDtypeStruct((part, width), dealt.dtype)] * 4
    return place_call(body, here, [dealt], shapes, "split_side")


def join_rows(pieces, here):
    part, width = pieces[0].shape

    def body(here, *refs):
        refs[4][...] = jnp.concatenate(
            [refs[here ^ i][...].astype(jnp.float32) for i in range(4)], axis=0
        ).astype(refs[4].dtype)

    shape = jax.ShapeDtypeStruct((4 * part, width), pieces[0].dtype)
    return place_call(body, here, pieces, [shape], "join_rows")[0]


def join_back(pieces, here, part):
    rows, count = pieces[0].shape
    runs = count // part

    def body(here, *refs):
        values = [ref[...].astype(jnp.float32) for ref in refs[:4]]
        refs[4][...] = jnp.concatenate(
            [
                values[here ^ i][:, r * part : (r + 1) * part]
                for r in range(runs)
                for i in range(4)
            ],
            axis=1,
        ).astype(refs[4].dtype)

    shape = jax.ShapeDtypeStruct((rows, 4 * count), pieces[0].dtype)
    return place_call(body, here, pieces, [shape], "join_back")[0]


def layout(lengths, buffer_rows):
    index = jnp.arange(lengths.shape[0], dtype=jnp.int32)
    count_blocks = (lengths + (BLOCK - 1)) // BLOCK
    earlier = (index[None, :] < index[:, None]).astype(jnp.int32)
    first_block = jnp.sum(earlier * count_blocks[None, :], axis=1)
    places = jnp.arange(buffer_rows, dtype=jnp.int32)
    owner = (
        jnp.sum((first_block[None, :] <= (places // BLOCK)[:, None]).astype(jnp.int32), axis=1) - 1
    )
    pick = (owner[:, None] == index[None, :]).astype(jnp.int32)
    seq_length = jnp.sum(pick * lengths[None, :], axis=1)
    offset = places - BLOCK * jnp.sum(pick * first_block[None, :], axis=1)
    live = offset < seq_length
    begins = live & (offset == 0)
    return (owner, offset, live, begins)


def product_tt(left, right):
    return lax.dot_general(
        left, right, (((0,), (1,)), ((), ())), preferred_element_type=jnp.float32
    )


def after(values, *others):
    return lax.optimization_barrier((values, others))[0]


def swap(values, bit):
    return lax.ppermute(values, "dp", [(i, i ^ bit) for i in range(4)])


def exchange(pieces):
    if len(pieces) != 4:
        return list(lax.all_to_all(jnp.stack(pieces), "dp", 0, 0))
    return [pieces[0]] + [swap(pieces[j], j) for j in (1, 2, 3)]


def trade(pieces):
    return lax.all_to_all(pieces, "dp", 0, 0)


def spread_direct(rows, groups):
    if groups != 4:
        return list(lax.all_gather(rows, "dp", axis=0))
    return [rows] + [swap(rows, j) for j in (1, 2, 3)]


def spread(rows, groups):
    if groups != 4:
        got = lax.all_gather(rows, "dp", axis=0, tiled=True)
        return got, got
    half = rows.shape[0] // 2
    one, two = swap(rows, 1), swap(rows, 2)
    far = [swap(one[:half], 2), swap(two[half:], 1)]
    return jnp.concatenate([rows, one, two] + far, axis=0), (one, two)


def first_hop(pieces):
    if len(pieces) != 4:
        return lax.all_to_all(jnp.stack(pieces), "dp", 0, 0)
    half = pieces[0].shape[0] // 2
    return (
        swap(pieces[3][:half], 1),
        swap(pieces[3][half:], 2),
        swap(pieces[1][:half], 1),
        swap(pieces[2][half:], 2),
    )


def second_hop(pieces, hops):
    wide, kind = jnp.float32, pieces[0].dtype
    if len(pieces) != 4:
        return jnp.sum(hops.astype(wide), axis=0)
    half = pieces[0].shape[0] // 2
    one_far, two_far, one, two = hops
    top = swap((pieces[2][:half].astype(wide) + one_far.astype(wide)).astype(kind), 2)
    bottom = swap((pieces[1][half:].astype(wide) + two_far.astype(wide)).astype(kind), 1)
    own = pieces[0].astype(wide)
    return jnp.concatenate(
        [
            own[:half] + one.astype(wide) + top.astype(wide),
            own[half:] + two.astype(wide) + bottom.astype(wide),
        ],
        axis=0,
    )


def collect(pieces):
    return second_hop(pieces, first_hop(pieces))


def whole_small(values, ranks):
    if ranks != 8:
        return lax.all_gather(values, "shard", axis=1, tiled=True)
    width = values.shape[1]
    slots = jnp.zeros((values.shape[0], ranks * width), values.dtype)
    slots = lax.dynamic_update_slice_in_dim(
        slots, values, lax.axis_index("shard") * width, axis=1
    )
    for step in (1, 2, 4):
        slots = slots + lax.ppermute(slots, "shard", [(i, i ^ step) for i in range(ranks)])
    return slots


def everyone(values, groups, ranks):
    if groups != 4:
        return lax.psum(values, ("dp", "shard"))
    values = values + swap(values, 1)
    values = values + swap(values, 2)
    step = 1
    while step < ranks:
        values = values + lax.ppermute(values, "shard", [(i, i ^ step) for i in range(ranks)])
        step *= 2
    return values


def row_pieces(partial, groups):
    rows = partial.shape[0] // groups
    return [partial[j * rows : (j + 1) * rows] for j in range(groups)]


def everywhere(partial, groups):
    if groups != 4:
        return lax.psum(partial, "dp")
    rows, width = partial.shape
    part = width // 4

    def turn(values, bit):
        return jnp.concatenate(
            [values[:, (j ^ bit) * part : ((j ^ bit) + 1) * part] for j in range(4)], axis=1
        )

    half = rows // 16 * 8
    top, bottom = partial[:half], partial[half:]
    top = top + swap(turn(top, 1), 1)
    bottom = bottom + swap(turn(bottom, 2), 2)
    top = top + swap(turn(top, 2), 2)
    bottom = bottom + swap(turn(bottom, 1), 1)
    return jnp.concatenate([top, bottom], axis=0)


def padded_part(part, ranks):
    unit = max(8, LANES // ranks)
    return -(-part // unit) * unit


def deal_columns(shard, here, groups, part, wide_part):
    rows, width = shard.shape
    runs = width // (groups * part)
    if groups == 4:
        starts = lambda i: [(r * groups + i) * part for r in range(runs)]
        pieces = exchange(split_columns(shard, here, starts, part))
        return join_columns(pieces, here, part, wide_part)
    pieces = shard.reshape(rows, runs, groups, part).transpose(2, 0, 1, 3)
    got = trade(pieces.reshape(groups, rows, runs * part)).transpose(1, 0, 2)
    got = jnp.pad(got.reshape(rows, groups * runs, part), ((0, 0), (0, 0), (0, wide_part - part)))
    return got.reshape(rows, groups * runs * wide_part)


def return_columns(dealt, here, groups, part, wide_part):
    rows, width = dealt.shape
    runs = width // (groups * wide_part)
    if groups == 4:
        starts = lambda i: [(i * runs + r) * wide_part for r in range(runs)]
        return join_back(exchange(split_columns(dealt, here, starts, part)), here, part)
    pieces = dealt.reshape(rows, groups * runs, wide_part)[:, :, :part]
    got = trade(pieces.reshape(rows, groups, runs * part).transpose(1, 0, 2))
    return got.reshape(groups, rows, runs, part).transpose(1, 2, 0, 3).reshape(rows, -1)


def deal_rows(shard, here, groups, wide_part):
    rows, width = shard.shape
    part = rows // groups
    if groups == 4:
        return join_side(exchange(split_rows(shard, here)), here, wide_part)
    got = trade(shard.reshape(groups, part, width))
    got = got.transpose(1, 0, 2).reshape(part, groups * width)
    return jnp.pad(got, ((0, wide_part - part), (0, 0)))


def return_rows(dealt, here, groups, part):
    width = dealt.shape[1]
    if groups == 4:
        return join_rows(exchange(split_side(dealt, here, part)), here)
    got = trade(dealt[:part].reshape(part, groups, width // groups).transpose(1, 0, 2))
    return got.reshape(groups * part, width // groups)


def beside(pieces, here):
    if len(pieces) != 4:
        return jnp.concatenate(pieces, axis=1)
    return join_side(pieces, here, pieces[0].shape[0])


def apart(values, here, groups):
    if groups != 4:
        return jnp.split(values, groups, axis=1)
    return split_side(values, here, values.shape[0])


def whole(shard):
    return lax.all_gather(shard, "shard", axis=0, tiled=True)


def owned_sum(partial):
    return lax.psum_scatter(partial, "shard", scatter_dimension=0, tiled=True)


def shards(
    groups,
    ranks,
    tokens,
    cotangent,
    lengths,
    step_count,
    norm_gains,
    qkv_weight,
    attn_weight,
    mixer_in,
    mixer_table,
    mixer_out,
    ffn_in,
    ffn_out,
    first_gains,
    first_qkv,
    first_attn,
    first_mixin,
    first_table,
    first_mixout,
    first_ffnin,
    first_ffnout,
    second_gains,
    second_qkv,
    second_attn,
    second_mixin,
    second_table,
    second_mixout,
    second_ffnin,
    second_ffnout,
):
    low = jnp.bfloat16
    buffer_rows = tokens.shape[0]
    model_width = tokens.shape[1]
    at = lax.axis_index("dp")
    here = at.reshape(1)
    part_inner = INNER // groups // ranks
    part_hidden = FF // groups // ranks
    wide_inner = padded_part(part_inner, ranks)
    wide_hidden = padded_part(part_hidden, ranks)
    inner = wide_inner * ranks
    hidden_units = wide_hidden * ranks
    part_model = model_width // ranks
    table_width = mixer_table.shape[1]
    gain_count = norm_gains.shape[1]

    qkv_width = qkv_weight.shape[1]
    attn_width = attn_weight.shape[1]
    table_part = lax.dynamic_slice_in_dim(mixer_table, at * part_inner, part_inner, axis=0)
    table_part = jnp.pad(
        table_part, ((0, part_model - part_inner), (0, 2 * LANES - table_width))
    )
    gain_cols = whole_small(norm_gains.astype(jnp.float32).T, ranks)
    mixer_pack = jnp.concatenate(
        [deal_columns(mixer_in, here, groups, part_inner, wide_inner), table_part, qkv_weight],
        axis=1,
    )
    mixer_early = whole(mixer_pack)
    lengths_all = jnp.concatenate(spread_direct(lengths, groups), axis=0)
    owner, offset, live, _ = layout(lengths[0], buffer_rows)
    live_rows = live.astype(jnp.float32)
    places = jnp.arange(buffer_rows, dtype=jnp.int32)
    allowed = (owner[:, None] == owner[None, :]) & (places[None, :] <= places[:, None]) & live[
        None, :
    ] | (places[:, None] == places[None, :])
    _, offset_all, _, begins_all = jax.vmap(lambda row: layout(row, buffer_rows))(lengths_all)
    offset_all = offset_all.reshape(-1)
    block_starts = begins_all[:, ::BLOCK] | (jnp.arange(buffer_rows // BLOCK) == 0)[None, :]
    block_keep = 1.0 - block_starts.reshape(-1).astype(jnp.float32)

    inputs = tokens.astype(jnp.float32)
    scale_in = rms_scale(inputs)
    normed = (inputs * scale_in * gain_cols[0]).astype(low)
    normed_all, near_rows = spread(after(normed, mixer_pack), groups)
    dealt_up = deal_columns(after(ffn_in, near_rows), here, groups, part_hidden, wide_hidden)
    dealt_rows = jnp.concatenate(
        [
            beside(spread_direct(attn_weight, groups), here),
            deal_rows(after(mixer_out, near_rows), here, groups, wide_inner),
            deal_rows(after(ffn_out, near_rows), here, groups, wide_hidden),
        ],
        axis=0,
    )
    mixer_full, normed_all, dealt_up, dealt_rows = lax.optimization_barrier(
        (mixer_early, normed_all, dealt_up, dealt_rows)
    )
    weight_in = mixer_full[:, : 2 * inner]
    weight_qkv = mixer_full[:, 2 * inner + 2 * LANES :]
    table_low = mixer_full[:, 2 * inner : 2 * inner + 2 * LANES].reshape(ranks, part_model, 2 * LANES)[:, :part_inner]
    table_low = jnp.pad(
        table_low[:, :, :table_width], ((0, 0), (0, wide_inner - part_inner), (0, 0))
    ).reshape(inner, table_width)

    rows_full = whole(dealt_rows).reshape(ranks, -1, model_width)
    mix_end = part_model + wide_inner
    weight_attn = rows_full[:, :part_model].reshape(model_width, model_width)
    weight_mix = rows_full[:, part_model:mix_end].reshape(inner, model_width)
    weight_down = rows_full[:, mix_end:].reshape(hidden_units, model_width)
    grad_out = cotangent.astype(jnp.float32) * live_rows[:, None]

    mixed = product(normed_all, weight_in)
    mixed, dealt_up = lax.optimization_barrier((mixed, dealt_up))
    weight_up = whole(dealt_up)
    table = table_low.astype(jnp.float32)
    channels = jnp.pad(table[:, : CONV + 3].T, ((0, 5 - CONV), (0, 0)))
    place = jnp.broadcast_to(offset_all[:, None], (offset_all.shape[0], LANES))
    conv_pre, conv_out, conv_low = conv_forward(mixed, place, channels)
    proj_start = CONV + 3 + STATE
    input_proj = table_low[:, proj_start : proj_start + RANK + 2 * STATE]
    step_proj = table_low[:, proj_start + RANK + 2 * STATE :]
    double_part = product_tt(input_proj, conv_low)
    double = everywhere(double_part, groups)

    heads_part = product(after(normed_all, double_part), weight_qkv).astype(low)
    heads_part = after(heads_part, double)
    heads_low = beside(exchange(row_pieces(heads_part, groups)), here)
    rank_part = double[:RANK].astype(low)
    inject = double[RANK : RANK + STATE]
    readout = double[RANK + STATE :]
    dt_pre = product_tt(rank_part, step_proj) + table[:, CONV + 1]
    step_size = jnp.log1p(jnp.exp(dt_pre))
    rates = -jnp.exp(table[:, CONV + 3 : CONV + 3 + STATE]).T
    scanned, gated_low, block_begins, inject_wide, readout_wide = scan_forward(
        block_keep, step_size, conv_out, inject, readout, rates, mixed, channels
    )
    gated_low, heads_low, grad_ffn_pieces = lax.optimization_barrier(
        (gated_low, heads_low, spread_direct(after(grad_out.astype(low), double), groups))
    )
    kv_width = KV * HEAD
    query = heads_low[:, :model_width].reshape(buffer_rows, KV, GROUP, HEAD)
    key_rows = heads_low[:, model_width : model_width + kv_width].reshape(buffer_rows, KV, HEAD)
    value_rows = heads_low[:, model_width + kv_width :].reshape(buffer_rows, KV, HEAD)
    factor = HEAD ** (-0.5)

    def masked_scores():
        raw_scores = (
            jnp.einsum("qkgd,skd->kgqs", query, key_rows, preferred_element_type=jnp.float32)
            * factor
        )
        return jnp.where(allowed, raw_scores, masked_score)

    scores = masked_scores()
    top_score = jnp.max(scores, axis=-1, keepdims=True)
    log_total = top_score + jnp.log(jnp.sum(jnp.exp(scores - top_score), axis=-1, keepdims=True))
    probs_low = jnp.exp(scores - log_total).astype(low)
    context = (
        jnp.einsum("kgqs,skd->qkgd", probs_low, value_rows, preferred_element_type=jnp.float32)
        .reshape(buffer_rows, model_width)
        .astype(low)
    )
    attn_raw = product(context, weight_attn)
    scale_attn = rms_scale(attn_raw)

    mamba_raw = collect(row_pieces(product(gated_low, weight_mix).astype(low), groups))
    mamba_raw = after(mamba_raw, attn_raw)
    scale_mamba = rms_scale(mamba_raw)
    hidden = inputs + 0.5 * (
        attn_raw * scale_attn * gain_cols[1] + mamba_raw * scale_mamba * gain_cols[2]
    )
    scale_hidden = rms_scale(hidden)
    normed_two = (hidden * scale_hidden * gain_cols[3]).astype(low)

    normed_two_all, _ = spread(normed_two, groups)
    both = product(normed_two_all, weight_up)
    grad_ffn_all = jnp.concatenate(grad_ffn_pieces, axis=0)
    gate_ffn = both[:, :hidden_units]
    up_ffn = both[:, hidden_units:]
    act_low = (silu_act(gate_ffn) * up_ffn).astype(low)
    grad_act = product_nt(grad_ffn_all, weight_down)
    gate_sig = sigmoid(gate_ffn)
    grad_gate = grad_act * up_ffn * gate_sig * (1.0 + gate_ffn * (1.0 - gate_sig))
    grad_up = grad_act * silu_act(gate_ffn)
    grad_both = jnp.concatenate([grad_gate, grad_up], axis=1).astype(low)
    grad_second = product_nt(grad_both, weight_up).astype(low)
    grad_up_w = product_tn(after(normed_two_all, grad_second), grad_both).astype(low)
    grad_down_w = product_tn(act_low, after(grad_ffn_all, grad_up_w)).astype(low)
    grad_second = collect(row_pieces(grad_second, groups))
    grad_second = after(grad_second, grad_up_w, grad_down_w)
    back_hidden, gain_three = rms_back(hidden, scale_hidden, gain_cols[3], grad_second)
    grad_hidden = grad_out + back_hidden
    half_grad = 0.5 * grad_hidden
    grad_mamba_full, gain_two = rms_back(mamba_raw, scale_mamba, gain_cols[2], half_grad)
    grad_mamba_all, _ = spread(grad_mamba_full.astype(low), groups)
    up_own = owned_sum(grad_up_w)

    grad_attn_full, gain_one = rms_back(attn_raw, scale_attn, gain_cols[1], half_grad)
    grad_attn_low = grad_attn_full.astype(low)
    grad_context = (
        product_nt(grad_attn_low, weight_attn).astype(low).reshape(buffer_rows, KV, GROUP, HEAD)
    )
    probs_again = jnp.exp(masked_scores() - log_total)
    grad_probs = jnp.einsum(
        "qkgd,skd->kgqs", grad_context, value_rows, preferred_element_type=jnp.float32
    )
    grad_values = jnp.einsum(
        "kgqs,qkgd->skd",
        probs_again.astype(low),
        grad_context,
        preferred_element_type=jnp.float32,
    )
    grad_scores = (
        probs_again * (grad_probs - jnp.sum(probs_again * grad_probs, axis=-1, keepdims=True))
    ).astype(low)
    grad_query = (
        jnp.einsum("kgqs,skd->qkgd", grad_scores, key_rows, preferred_element_type=jnp.float32)
        * factor
    )
    grad_keys = (
        jnp.einsum("kgqs,qkgd->skd", grad_scores, query, preferred_element_type=jnp.float32)
        * factor
    )
    grad_heads = jnp.concatenate(
        [
            grad_query.reshape(buffer_rows, model_width),
            grad_keys.reshape(buffer_rows, kv_width),
            grad_values.reshape(buffer_rows, kv_width),
        ],
        axis=1,
    ).astype(low)
    head_pieces = exchange(apart(grad_heads, here, groups))

    grad_attn_w = product_tn(context, grad_attn_low).astype(low)
    grad_mamba_all, grad_heads, grad_attn_w = lax.optimization_barrier(
        (grad_mamba_all, grad_heads, grad_attn_w)
    )
    down_own, attn_own = owned_sum(grad_down_w), owned_sum(grad_attn_w)
    grad_gated = product_nt(grad_mamba_all, weight_mix)
    grad_mix_w = product_tn(gated_low, grad_mamba_all).astype(low)
    raw_pieces = row_pieces(product(after(act_low, grad_gated), weight_down).astype(low), groups)
    grad_gated, raw_pieces, grad_mix_w = lax.optimization_barrier(
        (grad_gated, raw_pieces, grad_mix_w)
    )
    mix_own = owned_sum(grad_mix_w)
    raw_hops = first_hop(raw_pieces)
    (
        grad_scanned,
        grad_gate_low,
        grad_pre_low,
        grad_conv_scan,
        grad_inject,
        grad_readout,
        grad_rates,
        scan_sums,
    ) = scan_backward(
        block_keep,
        step_size,
        conv_out,
        inject_wide,
        readout_wide,
        rates,
        grad_gated,
        mixed,
        scanned,
        dt_pre,
        block_begins,
    )
    grad_pre_low, raw_hops, head_pieces = lax.optimization_barrier(
        (grad_pre_low, raw_hops, head_pieces)
    )
    grad_heads_part = jnp.concatenate(head_pieces, axis=0)
    grad_rank = product_tt(step_proj, grad_pre_low)
    grad_double = everywhere(
        jnp.concatenate([grad_rank, grad_inject, grad_readout], axis=0), groups
    ).astype(low)

    raw_hops = after(raw_hops, grad_double)
    ffn_raw = second_hop(raw_pieces, raw_hops)
    output = (live_rows[:, None] * (hidden + ffn_raw)).astype(low)
    side_pack = jnp.concatenate(
        [
            product_tn(normed_all, grad_heads_part).astype(low),
            product_tn(normed_all, grad_gate_low).astype(low),
        ],
        axis=1,
    )
    side_pack, grad_double = lax.optimization_barrier((side_pack, grad_double))
    side_own = owned_sum(side_pack)
    conv_part = product_tt(grad_double, input_proj)
    conv_part, up_own, down_own, attn_own = lax.optimization_barrier(
        (conv_part, up_own, down_own, attn_own)
    )
    grad_xin_low, conv_sums = conv_backward(
        conv_part, grad_conv_scan, grad_scanned, conv_pre, mixed, place, channels
    )
    grad_table = jnp.concatenate(
        [
            conv_sums[: CONV + 1],
            scan_sums[1:2],
            scan_sums[0:1],
            grad_rates * rates,
            product(grad_double, conv_low),
            product(rank_part, grad_pre_low),
            jnp.zeros((2 * LANES - table_width, inner), jnp.float32),
        ],
        axis=0,
    ).astype(low)
    grad_table = jnp.pad(
        grad_table.T.reshape(ranks, wide_inner, 2 * LANES),
        ((0, 0), (0, part_model - wide_inner), (0, 0)),
    ).reshape(model_width, 2 * LANES)
    xin_pack = jnp.concatenate(
        [product_tn(normed_all, grad_xin_low).astype(low), grad_table], axis=1
    )
    xin_pack, mix_own = lax.optimization_barrier((xin_pack, mix_own))
    last_own = owned_sum(xin_pack)
    normed_part = (
        product_nt(grad_heads_part, weight_qkv)
        + product_nt(grad_gate_low, weight_in[:, inner:])
        + product_nt(after(grad_xin_low, xin_pack), weight_in[:, :inner])
    )
    gain_zero = jnp.sum(normed_part * normed_all.astype(jnp.float32), axis=0) / gain_cols[0]
    normed_part, up_own = lax.optimization_barrier((normed_part.astype(low), up_own))
    if groups == 4:
        runs = 2 * ranks // groups
        starts = lambda i: [(i * runs + r) * wide_hidden for r in range(runs)]
        up_pieces = exchange(split_columns(up_own, here, starts, part_hidden))
    else:
        up_pieces = return_columns(up_own, here, groups, part_hidden, wide_hidden)
    up_done = join_back(up_pieces, here, part_hidden) if groups == 4 else up_pieces
    grad_normed = collect(row_pieces(normed_part, groups))
    grad_normed, side_own = lax.optimization_barrier((grad_normed, side_own))
    back_inputs, _ = rms_back(inputs, scale_in, gain_cols[0], grad_normed)
    grad_tokens = grad_hidden + back_inputs
    grad_gains = everyone(jnp.stack([gain_zero, gain_one, gain_two, gain_three], axis=0), groups, ranks)
    grad_gains_done = lax.dynamic_slice_in_dim(
        grad_gains, lax.axis_index("shard") * part_model, part_model, axis=1
    ).T

    last_own = lax.optimization_barrier(last_own)
    side_own = lax.optimization_barrier(side_own)
    grad_in_done = return_columns(
        jnp.concatenate([last_own[:, :inner], side_own[:, qkv_width:]], axis=1),
        here,
        groups,
        part_inner,
        wide_inner,
    )
    table_pieces = spread_direct(last_own[:part_inner, inner : inner + 2 * LANES], groups)
    if groups == 4:
        grad_table_done = join_rows(table_pieces, here)[:, :table_width]
    else:
        grad_table_done = jnp.concatenate(table_pieces, axis=0)[:, :table_width]
    grad_qkv_done = side_own[:, :qkv_width]
    grad_attn_done = sum(
        piece.astype(jnp.float32)
        for piece in exchange(apart(attn_own, here, groups))
    )
    grad_mix_done = return_rows(after(mix_own, normed_part), here, groups, part_inner)
    ffn_done = (
        up_done,
        return_rows(after(down_own, normed_part), here, groups, part_hidden),
    )

    owned = (norm_gains, qkv_weight, attn_weight, mixer_in, mixer_table, mixer_out, ffn_in, ffn_out)
    grads_owned = (
        grad_gains_done,
        grad_qkv_done,
        grad_attn_done,
        grad_in_done,
        grad_table_done,
        grad_mix_done,
        ffn_done[0],
        ffn_done[1],
    )
    firsts = (
        first_gains,
        first_qkv,
        first_attn,
        first_mixin,
        first_table,
        first_mixout,
        first_ffnin,
        first_ffnout,
    )
    seconds = (
        second_gains,
        second_qkv,
        second_attn,
        second_mixin,
        second_table,
        second_mixout,
        second_ffnin,
        second_ffnout,
    )
    step_float = step_count[0].astype(jnp.float32)
    updates = [
        adam_rows(owned[slot], grads_owned[slot], firsts[slot], seconds[slot], step_float)
        for slot in range(8)
    ]
    return (output, grad_tokens) + tuple(entry[kind] for kind in range(4) for entry in updates)


def solution(mesh):
    in_specs = (
        P(("dp", "shard"), None),
        P(("dp", "shard"), None),
        P(("dp", "shard"), None),
        P(),
        P("shard", None),
        P("shard", "dp"),
        P("shard", "dp"),
        P("shard", "dp"),
        P("shard", None),
        P("shard", "dp"),
        P("shard", "dp"),
        P("shard", "dp"),
        P("shard", None),
        P("shard", "dp"),
        P("shard", "dp"),
        P("shard", "dp"),
        P("shard", None),
        P("shard", "dp"),
        P("shard", "dp"),
        P("shard", "dp"),
        P("shard", None),
        P("shard", "dp"),
        P("shard", "dp"),
        P("shard", "dp"),
        P("shard", None),
        P("shard", "dp"),
        P("shard", "dp"),
        P("shard", "dp"),
    )
    out_specs = (
        P(("dp", "shard"), None),
        P(("dp", "shard"), None),
        P("shard", None),
        P("shard", "dp"),
        P("shard", "dp"),
        P("shard", "dp"),
        P("shard", None),
        P("shard", "dp"),
        P("shard", "dp"),
        P("shard", "dp"),
        P("shard", None),
        P("shard", "dp"),
        P("shard", "dp"),
        P("shard", "dp"),
        P("shard", None),
        P("shard", "dp"),
        P("shard", "dp"),
        P("shard", "dp"),
        P("shard", None),
        P("shard", "dp"),
        P("shard", "dp"),
        P("shard", "dp"),
        P("shard", None),
        P("shard", "dp"),
        P("shard", "dp"),
        P("shard", "dp"),
        P("shard", None),
        P("shard", "dp"),
        P("shard", "dp"),
        P("shard", "dp"),
        P("shard", None),
        P("shard", "dp"),
        P("shard", "dp"),
        P("shard", "dp"),
    )
    return jax.shard_map(functools.partial(shards, mesh.shape["dp"], mesh.shape["shard"]), mesh=mesh, in_specs=in_specs, out_specs=out_specs, check_vma=False)
```
